128 devices in a mesh: lon: 16 (over y_lo, z, core), filt: 8 (over y_hi, x).
Axes of the slice: x: 4, y: 4 (y_hi: 2, y_lo: 2; y = y_hi * 2 + y_lo), z: 4, core: 2. Of those that a mesh axis runs over, the one named last changes fastest.
Arguments:
- ocean_state: bfloat16 [256, 16, 4096], P(None, None, 'lon'), may hold values from -6 to 6
- cotangent: bfloat16 [256, 16, 4096], P(None, None, 'lon'), may hold values from -6 to 6
- conv_in: bfloat16 [9, 256, 1024], P(None, None, 'filt'), may hold values from -0.1875 to 0.1875
- conv_out: bfloat16 [9, 1024, 256], P(None, 'filt'), may hold values from -0.09375 to 0.09375
- tile_mask: int32 [2, 32], replicated, may hold values from 0 to 1, as said below
Outputs:
- block_out: bfloat16 [256, 16, 4096], P('filt', None, 'lon')
- grad_state: bfloat16 [256, 16, 4096], P('filt', None, 'lon')
- grad_conv_in: float32 [9, 256, 1024], P(None, None, 'filt')
- grad_conv_out: float32 [9, 1024, 256], P(None, 'filt')
The draws below stay inside these ranges and needn't reach their ends.
Inputs may be any that keep to these rules, and one draw needn't show every extreme that they name: `tile_mask`: 1 marks an ocean tile of 8 x 128 cells, 0 a land tile; every tile of the first tile row is ocean, and the last tile row holds land.
All inputs are finite; a program needn't handle non-finite values.
Results may differ from the reference program's by a relative error of at most 0.0037.
Values may be sent and summed in bfloat16 or wider, within the bound.
A program may use at most 192 MiB of HBM per device.

```python
import math
import jax
import jax.numpy as jnp

C = 256
MID = 1024
ROWS = 16
TILE_H = 8
TILE_W = 128
W = 4096


def draw_tile_mask(key, part):
    key = jax.random.fold_in(key, 7)
    tile_rows = ROWS // TILE_H
    tile_cols = W // TILE_W
    first_key, second_key = jax.random.split(key)
    coins = jax.random.randint(first_key, (tile_rows, tile_cols), 0, 2)
    tile_row_ids = jnp.arange(tile_rows, dtype=jnp.int32)[:, None]
    tile_col_ids = jnp.arange(tile_cols, dtype=jnp.int32)[None, :]
    land_col = jax.random.randint(second_key, (), 0, tile_cols)
    forced_land = (tile_row_ids == tile_rows - 1) & (tile_col_ids == land_col)
    ocean = jnp.where(tile_row_ids == 0, 1, coins)
    ocean = jnp.where(forced_land, 0, ocean)
    return ocean.astype(jnp.int32)


def raised(entries, stream_key, source, target, blocks, factor):
    owner, partner = [(jnp.arange(entries.shape[axis_at]) // (entries.shape[axis_at] // blocks)).reshape([-1 if axis == axis_at else 1 for axis in range(entries.ndim)]) for axis_at in (source, target)]
    chosen = jax.random.permutation(stream_key, blocks)[partner]
    strong = (owner == chosen) | (owner == (partner + blocks // 2) % blocks)
    return jnp.where(strong, factor * entries, entries)


def steps_of(key, dims, cuts, least, high):
    level, own = 1.0, jax.random.fold_in(key, 6)
    for axis_at, blocks in cuts:
        steps = jnp.exp(jax.random.uniform(jax.random.fold_in(own, axis_at), (blocks,), jnp.float32, least / len(cuts), high / len(cuts)))
        level = level * jnp.repeat(steps, dims[axis_at] // blocks).reshape([-1 if axis == axis_at else 1 for axis in range(len(dims))])
    return level


def gaussian(key, extent, scale, most, cuts=(), held_as=jnp.bfloat16):
    result = jax.random.normal(key, extent, jnp.float32) * scale
    if len(cuts) > 0:
        result = steps_of(key, extent, cuts, -0.22, 0.18) * result
    return jnp.clip(result, min=-most, max=most).astype(held_as)


def bell_draw_with(key, dims, scale, limit, cuts, heavy, kind=jnp.bfloat16):
    values = scale * jax.random.normal(key, dims, jnp.float32)
    if cuts:
        values = values * steps_of(key, dims, cuts, -0.22, 0.18)
    return jnp.clip(raised(values, jax.random.fold_in(key, 3), *heavy), -limit, limit).astype(kind)


def setup_inputs(seed: int = 0) -> dict:
    seeds = jax.random.split(jax.random.key(seed), 6)
    ocean_state = gaussian(seeds[0], (C, ROWS, W), 1.0, 6.0, ((2, 16),))
    cotangent = gaussian(seeds[1], (C, ROWS, W), 1.0, 6.0, ((2, 16),))
    conv_in = bell_draw_with(seeds[2], (9, C, MID), (9 * C) ** -0.5, 0.1875, ((2, 8),), (2, 1, 8, 2.0))
    conv_out = bell_draw_with(seeds[3], (9, MID, C), (9 * MID) ** -0.5, 0.09375, ((1, 8),), (1, 2, 8, 2.0))
    tile_mask = draw_tile_mask(jax.random.fold_in(seeds[5], 71), 0)
    return dict(ocean_state=ocean_state, cotangent=cotangent, conv_in=conv_in, conv_out=conv_out, tile_mask=tile_mask)


root_half = 0.7071067811865476
norm_const = 0.3989422804014327

def gelu_grad(values):
    return 0.5 * (1.0 + jax.lax.erf(values * root_half)) + values * jnp.exp(-0.5 * values * values) * norm_const

def wrap_pad(values):
    wide = jnp.concatenate([values[:, :, -1:], values, values[:, :, :1]], axis=2)
    return jnp.pad(wide, ((0, 0), (1, 1), (0, 0)))

def conv_apply(padded, weights, flipped, height, breadth):
    summed = None
    for offset in range(9):
        row_off, col_off = (offset // 3, offset % 3)
        if flipped:
            row_off, col_off = (2 - row_off, 2 - col_off)
        window = padded[:, row_off:row_off + height, col_off:col_off + breadth]
        matrix = weights[offset] if flipped else weights[offset].T
        partial_value = jnp.dot(matrix, window.reshape(window.shape[0], -1), preferred_element_type=jnp.float32)
        summed = partial_value if summed is None else summed + partial_value
    return summed.reshape(-1, height, breadth)

def weight_grads(padded, target, height, breadth):
    flat_target = target.reshape(target.shape[0], -1).T
    results = []
    for offset in range(9):
        row_off, col_off = (offset // 3, offset % 3)
        window = padded[:, row_off:row_off + height, col_off:col_off + breadth]
        results.append(jnp.dot(window.reshape(window.shape[0], -1), flat_target, preferred_element_type=jnp.float32))
    return jnp.stack(results, 0)

def reference(ocean_state, cotangent, conv_in, conv_out, tile_mask):
    height, breadth = (ocean_state.shape[1], ocean_state.shape[2])
    ocean_cells = jnp.repeat(jnp.repeat(tile_mask.astype(jnp.float32), TILE_H, 0), TILE_W, 1)
    cell_half = ocean_cells.astype(jnp.bfloat16)
    state_masked = ocean_state * cell_half
    state_pad = wrap_pad(state_masked)
    pre_act = conv_apply(state_pad, conv_in, False, height, breadth)
    hidden = (ocean_cells * jax.nn.gelu(pre_act, approximate=False)).astype(jnp.bfloat16)
    hidden_pad = wrap_pad(hidden)
    mixed_sum = conv_apply(hidden_pad, conv_out, False, height, breadth)
    block_out = (ocean_state + ocean_cells * mixed_sum).astype(jnp.bfloat16)
    cot_masked = cotangent * cell_half
    grad_hidden = conv_apply(wrap_pad(cot_masked), conv_out, True, height, breadth)
    grad_pre = (grad_hidden * gelu_grad(pre_act) * ocean_cells).astype(jnp.bfloat16)
    back_sum = conv_apply(wrap_pad(grad_pre), conv_in, True, height, breadth)
    grad_state = (cotangent + ocean_cells * back_sum).astype(jnp.bfloat16)
    grad_scale = 1.0 / math.sqrt(height * breadth)
    grad_conv_in = weight_grads(state_pad, grad_pre, height, breadth) * grad_scale
    grad_conv_out = weight_grads(hidden_pad, cot_masked, height, breadth) * grad_scale
    return (block_out, grad_state, grad_conv_in, grad_conv_out)
```

```python
import functools

import jax
import jax.numpy as jnp
from jax import lax
from jax.experimental import pallas as pl
from jax.experimental.pallas import tpu as pltpu
from jax.sharding import PartitionSpec as P

TILE_H = 8
TILE_W = 128
MESH = pl.DeviceIdType.MESH
BF = jnp.bfloat16
F32 = jnp.float32
ROOT_HALF = 0.7071067811865476
NORM_CONST = 0.3989422804014327


def dot(a, b):
    return lax.dot_general(a, b, (((1,), (0,)), ((), ())), preferred_element_type=F32)


def dot_t(a, b):
    return lax.dot_general(a, b, (((1,), (1,)), ((), ())), preferred_element_type=F32)


def gelu_parts(v):
    e = 0.5 * (1.0 + lax.erf(v * ROOT_HALF))
    return v * e, e + v * jnp.exp(-0.5 * v * v) * NORM_CONST


def coords():
    lon, filt = lax.axis_index("lon"), lax.axis_index("filt")
    y, x = filt // 4, filt % 4
    v = x // 2
    u = (x + v) % 2
    return lon, filt, u, v, y


def filt_of(u, v, y):
    return 4 * y + 2 * v + (u + v) % 2


def kernel(
    x_ref, c_ref, xh_ref, ch_ref, w1_ref, w2_ref, w3_ref, w4_ref, mask_ref, maskh_ref,
    sums_ref, grads_ref,
    hs, gps, edge, hedge, keep, s1, r1, s2, r2, s3, r3,
    gacc, gx, gxr, gsum, gs, gr, gall, goth,
    send_sem, recv_sem, gxs_sem, gxr_sem, gs_sem, gr_sem, ga_sem, gar_sem, go_sem, gor_sem, out_sem,
):
    lon, filt, u, v, y = coords()
    core = lon % 2
    chip = lon // 2
    lane256 = lax.broadcasted_iota(jnp.int32, (128, 256), 1)
    partners = ((lon, filt_of(1 - u, v, y)), (lon, filt_of(u, 1 - v, y)), (lon, filt_of(u, v, 1 - y)))
    mate = (chip * 2 + (1 - core), filt)

    def peer(d):
        z, yl = chip % 4, chip // 4
        z = (z + d % 4) % 4
        yl = (yl + d // 4) % 2
        return yl * 4 + z

    def opposite(d):
        return (4 - d % 4) % 4 + (d // 4) * 4

    barrier = pltpu.get_barrier_semaphore()
    for who in partners + (mate,):
        pl.semaphore_signal(barrier, inc=1, device_id=who, device_id_type=MESH)
    for d in range(1, 8):
        pl.semaphore_signal(barrier, inc=1, device_id=(peer(d) * 2 + core, filt), device_id_type=MESH)

    lane_h = lax.broadcasted_iota(jnp.int32, (384, 128), 1) % 16

    def halo(w_ref, t_ref):
        total = dot(w_ref[:, 256:512], t_ref[...])
        above = pltpu.roll(dot(w_ref[:, 0:256], t_ref[...]), 1, 1)
        below = pltpu.roll(dot(w_ref[:, 512:768], t_ref[...]), 127, 1)
        return total + jnp.where(lane_h == 0, 0.0, above) + jnp.where(lane_h == 15, 0.0, below)

    def halo_mid(s):
        return pltpu.roll(s[0:128], 16, 1) + s[128:256] + pltpu.roll(s[256:384], 112, 1)

    sp = halo(w1_ref, xh_ref)
    sg = halo(w2_ref, ch_ref)
    edge[0] = sp[0:128]
    edge[1] = sp[256:384]
    edge[2] = sg[0:128]
    edge[3] = sg[256:384]
    act, slope = gelu_parts(halo_mid(sp))
    hedge[0] = act * maskh_ref[...]
    hedge[1] = halo_mid(sg) * slope * maskh_ref[...]
    for ref in (hs, gps):
        ref[0] = jnp.zeros((384, 256), BF)
        ref[17] = jnp.zeros((384, 256), BF)

    def to_left(tile, row):
        moved = pltpu.roll(tile, 112 - row, 1)
        return jnp.concatenate([moved, moved], axis=1)

    def to_right(tile, row):
        moved = pltpu.roll(tile, 63 - row, 1)
        return jnp.concatenate([moved, moved], axis=1)

    def before(val, tile, row):
        return jnp.where(lane256 == 0, to_left(tile, row), pltpu.roll(val, 1, 1))

    def after(val, tile, row):
        return jnp.where(lane256 == 255, to_right(tile, row), pltpu.roll(val, 255, 1))

    def two_rows(ref, row, height):
        return jnp.concatenate(
            [ref[pl.ds(row, 3)].reshape(3 * height, 256), ref[pl.ds(row + 1, 3)].reshape(3 * height, 256)], axis=1
        )

    def first_stage(q):
        row0 = 2 * q
        zp = dot(w1_ref[...], two_rows(x_ref, row0, 256))
        zg = dot(w2_ref[...], two_rows(c_ref, row0, 256))
        for s in range(2):
            row = row0 + s
            a = zp[:, 256 * s : 256 * s + 256]
            b = zg[:, 256 * s : 256 * s + 256]
            pre = a[128:256] + before(a[0:128], edge[0], row) + after(a[256:384], edge[1], row)
            gh = b[128:256] + before(b[0:128], edge[2], row) + after(b[256:384], edge[3], row)
            mask = mask_ref[row]
            act, slope = gelu_parts(pre)
            for ref, val, tile in ((hs, act * mask, hedge[0]), (gps, gh * slope * mask, hedge[1])):
                ref[row + 1, 0:128] = before(val, tile, row).astype(BF)
                ref[row + 1, 128:256] = val.astype(BF)
                ref[row + 1, 256:384] = after(val, tile, row).astype(BF)

    bufs = ((s1, r1), (s2, r2), (s3, r3))
    order = ((0, 2, 1), (1, 2, 0))

    def hop(step, a, q):
        src, dst = bufs[step]
        return pltpu.make_async_remote_copy(
            src_ref=src.at[a, q], dst_ref=dst.at[a, q], send_sem=send_sem.at[step, a, q], recv_sem=recv_sem.at[step, a, q],
            device_id=partners[order[a][step]], device_id_type=MESH,
        )

    def second_stage(q):
        for a, (w_ref, ref) in enumerate(((w3_ref, hs), (w4_ref, gps))):
            res = dot(w_ref[...], two_rows(ref, 2 * q, 384))
            for s in range(2):
                part = res[:, 256 * s : 256 * s + 256]
                keep[a, q, s] = part[0:128]
                s1[a, q, s] = part[128:256].astype(BF)
            hop(0, a, q).start()

    def advance(step, q):
        left = (64, 32, 0)[step]
        for a in range(2):
            hop(step, a, q).wait_recv()
            for s in range(2):
                got = bufs[step][1][a, q, s].astype(F32)
                if step < 2:
                    total = keep[a, q, s, 0 : 2 * left] + got
                    keep[a, q, s, 0:left] = total[0:left]
                    bufs[step + 1][0][a, q, s] = total[left : 2 * left].astype(BF)
                else:
                    sums_ref[a, 2 * q + s] = keep[a, q, s, 0:32] + got
            if step < 2:
                hop(step + 1, a, q).start()

    def progress(t):
        for step, lag in enumerate((3, 5, 7)):
            @pl.when((t >= lag) & (t < lag + 8))
            def _():
                advance(step, t - lag)

    @pl.loop(0, 9)
    def _(t):
        @pl.when(t < 8)
        def _():
            first_stage(t)

        @pl.when(t == 1)
        def _():
            pl.semaphore_wait(barrier, 11)

        @pl.when(t >= 1)
        def _():
            second_stage(t - 1)

        progress(t)

    def to_mate(g):
        return pltpu.make_async_remote_copy(
            src_ref=gx.at[g], dst_ref=gxr.at[g], send_sem=gxs_sem.at[g], recv_sem=gxr_sem.at[g],
            device_id=mate, device_id_type=MESH,
        )

    def scatter(g, d):
        return pltpu.make_async_remote_copy(
            src_ref=gs.at[g, peer(d)], dst_ref=gr.at[g, d], send_sem=gs_sem.at[g, d], recv_sem=gr_sem.at[g, d],
            device_id=(peer(d) * 2 + core, filt), device_id_type=MESH,
        )

    def spread(g, d):
        return pltpu.make_async_remote_copy(
            src_ref=gall.at[g, chip], dst_ref=gall.at[g, chip], send_sem=ga_sem.at[g, d], recv_sem=gar_sem.at[g, d],
            device_id=(peer(d) * 2 + core, filt), device_id_type=MESH,
        )

    def arrival(g, d):
        return pltpu.make_async_remote_copy(
            src_ref=gall.at[g, chip], dst_ref=gall.at[g, peer(opposite(d))], send_sem=ga_sem.at[g, d], recv_sem=gar_sem.at[g, d],
            device_id=(peer(d) * 2 + core, filt), device_id_type=MESH,
        )

    def across(g):
        return pltpu.make_async_remote_copy(
            src_ref=gall.at[g], dst_ref=goth.at[g], send_sem=go_sem.at[g], recv_sem=gor_sem.at[g],
            device_id=mate, device_id_type=MESH,
        )

    def weight_round(g):
        for a, (ref, other) in enumerate(((hs, c_ref), (gps, x_ref))):
            gacc[a] = jnp.zeros((384, 256), F32)

            @pl.loop(0, 4)
            def _(b):
                left = jnp.concatenate([ref[4 * b + j + g] for j in range(4)], axis=1)
                right = jnp.concatenate([other[4 * b + j + 1] for j in range(4)], axis=1)
                gacc[a] += dot_t(left, right)
        gx[g] = gacc[1 - core].astype(BF)
        to_mate(g).start()

    def gather_mate(g):
        to_mate(g).wait_recv()
        total = gacc[core] + gxr[g].astype(F32)
        total = total.reshape(8, 48, 256)
        gsum[g] = total
        gs[g] = total.astype(BF)
        for d in range(1, 8):
            scatter(g, d).start()

    def finish_piece(g):
        total = gsum[g, chip]
        for d in range(1, 8):
            scatter(g, d).wait_recv()
            total = total + gr[g, d].astype(F32)
        gall[g, chip] = total.astype(BF)
        for d in range(1, 8):
            spread(g, d).start()

    def swap_cores(g):
        for d in range(1, 8):
            arrival(g, d).wait_recv()
        across(g).start()

    @pl.loop(0, 3)
    def _(g):
        weight_round(g)

        @pl.when(g >= 1)
        def _():
            finish_piece(g - 1)

        progress(9 + 2 * g)
        gather_mate(g)
        progress(10 + 2 * g)

        @pl.when(g >= 1)
        def _():
            swap_cores(g - 1)

    finish_piece(2)
    swap_cores(2)
    for g in range(3):
        across(g).wait_recv()
    own = pltpu.make_async_copy(gall, grads_ref.at[core], out_sem.at[0])
    oth = pltpu.make_async_copy(goth, grads_ref.at[1 - core], out_sem.at[1])
    own.start()
    oth.start()

    @pl.loop(0, 8)
    def _(q):
        for step in range(3):
            for a in range(2):
                hop(step, a, q).wait_send()

    @pl.loop(0, 3)
    def _(g):
        to_mate(g).wait_send()
        across(g).wait_send()
        for d in range(1, 8):
            scatter(g, d).wait_send()
            spread(g, d).wait_send()

    own.wait()
    oth.wait()


def call_kernel(*args):
    vm = pltpu.VMEM
    dma = pltpu.SemaphoreType.DMA
    whole = pl.BlockSpec(memory_space=pltpu.VMEM)
    return pl.pallas_call(
        kernel,
        name="ocean_block",
        out_shape=(
            jax.ShapeDtypeStruct((2, 16, 32, 256), F32),
            jax.ShapeDtypeStruct((2, 3, 8, 48, 256), BF),
        ),
        in_specs=[whole] * 10,
        out_specs=(whole, pl.BlockSpec(memory_space=pl.ANY)),
        scratch_shapes=[
            vm((18, 384, 256), BF), vm((18, 384, 256), BF), vm((4, 128, 128), F32), vm((2, 128, 128), F32),
            vm((2, 8, 2, 128, 256), F32),
            vm((2, 8, 2, 128, 256), BF), vm((2, 8, 2, 128, 256), BF),
            vm((2, 8, 2, 64, 256), BF), vm((2, 8, 2, 64, 256), BF),
            vm((2, 8, 2, 32, 256), BF), vm((2, 8, 2, 32, 256), BF),
            vm((2, 384, 256), F32), vm((3, 384, 256), BF), vm((3, 384, 256), BF),
            vm((3, 8, 48, 256), F32), vm((3, 8, 48, 256), BF), vm((3, 8, 48, 256), BF),
            vm((3, 8, 48, 256), BF), vm((3, 8, 48, 256), BF),
            dma((3, 2, 8)), dma((3, 2, 8)), dma((3,)), dma((3,)), dma((3, 8)), dma((3, 8)), dma((3, 8)), dma((3, 8)),
            dma((3,)), dma((3,)), dma((2,)),
        ],
        compiler_params=pltpu.CompilerParams(
            collective_id=1, has_side_effects=True, vmem_limit_bytes=56 * 2**20
        ),
        cost_estimate=pl.CostEstimate(flops=14_500_000_000, bytes_accessed=10_000_000, transcendentals=1_000_000),
    )(*args)


def shards(ocean_state, cotangent, conv_in, conv_out, tile_mask):
    channels, height, breadth = ocean_state.shape
    lon, filt, u, v, y = coords()
    peers = lax.axis_size("lon")
    tiles = tile_mask.shape[1]
    per_dev = breadth // TILE_W
    wide = lax.dynamic_slice_in_dim(
        jnp.concatenate([tile_mask[:, -1:], tile_mask, tile_mask[:, :1]], axis=1), lon * per_dev, per_dev + 2, 1
    ).astype(F32)
    rows = jnp.repeat(wide, TILE_H, axis=0)
    mask = jnp.repeat(rows[:, 1:-1], TILE_W, axis=1)
    maskh = jnp.concatenate(
        [rows[:, 0], rows[:, 0], rows[:, 1], rows[:, -2], rows[:, -1], rows[:, -1], jnp.zeros((32,), F32)]
    )[None, :]

    first = jnp.concatenate([ocean_state[:, :, 0:2], cotangent[:, :, 0:2]], axis=0)
    last = jnp.concatenate([ocean_state[:, :, -2:], cotangent[:, :, -2:]], axis=0)
    first = jnp.swapaxes(first, 1, 2).reshape(2 * channels, 2 * height)
    last = jnp.swapaxes(last, 1, 2).reshape(2 * channels, 2 * height)
    up = [(i, (i + 1) % peers) for i in range(peers)]
    down = [(j, i) for i, j in up]
    left = lax.ppermute(last, "lon", up)
    right = lax.ppermute(first, "lon", down)
    edges = jnp.concatenate(
        [left, first[:, 0:height], last[:, height:], right, jnp.zeros((2 * channels, 32), BF)], axis=1
    ) * maskh.astype(BF)

    mask_bf = mask.astype(BF)

    def by_row(t):
        return jnp.pad(jnp.swapaxes(t * mask_bf, 0, 1), ((1, 1), (0, 0), (0, 0)))

    k_in = conv_in.reshape(3, 3, 256, 128)
    k_out = conv_out.reshape(3, 3, 128, 256)
    w1 = jnp.transpose(k_in, (1, 3, 0, 2)).reshape(384, 768)
    w2 = jnp.transpose(k_out[::-1, ::-1], (1, 2, 0, 3)).reshape(384, 768)
    w3 = jnp.transpose(conv_out, (2, 0, 1)).reshape(8, 32, 1152)
    w4 = jnp.transpose(conv_in[::-1], (1, 0, 2)).reshape(8, 32, 1152)
    w3 = jnp.concatenate(
        [
            lax.dynamic_slice_in_dim(w3, filt_of((u + i) % 2, (v + k) % 2, (y + j) % 2), 1, 0)
            for i in range(2) for j in range(2) for k in range(2)
        ]
    ).reshape(256, 1152)
    w4 = jnp.concatenate(
        [
            lax.dynamic_slice_in_dim(w4, filt_of((u + k) % 2, (v + i) % 2, (y + j) % 2), 1, 0)
            for i in range(2) for j in range(2) for k in range(2)
        ]
    ).reshape(256, 1152)

    sums, grads = call_kernel(
        by_row(ocean_state), by_row(cotangent), edges[:channels], edges[channels:], w1, w2, w3, w4,
        mask[:, None, :], maskh,
    )
    own = channels // lax.axis_size("filt")
    state_own = lax.dynamic_slice_in_dim(ocean_state, filt * own, own, 0)
    cot_own = lax.dynamic_slice_in_dim(cotangent, filt * own, own, 0)
    block_out = (state_own + mask * jnp.swapaxes(sums[0], 0, 1)).astype(BF)
    grad_state = (cot_own + mask * jnp.swapaxes(sums[1], 0, 1)).astype(BF)
    scale = 1.0 / (height * breadth * peers) ** 0.5
    grads = grads.reshape(2, 9, 128, 256)
    grad_out = grads[0].astype(F32) * scale
    grad_in = jnp.swapaxes(grads[1][::-1], 1, 2).astype(F32) * scale
    return (block_out, grad_state, grad_in, grad_out)


def solution(mesh):
    in_specs = (
        P(None, None, "lon"),
        P(None, None, "lon"),
        P(None, None, "filt"),
        P(None, "filt", None),
        P(),
    )
    out_specs = (
        P("filt", None, "lon"),
        P("filt", None, "lon"),
        P(None, None, "filt"),
        P(None, "filt", None),
    )
    return jax.shard_map(shards, mesh=mesh, in_specs=in_specs, out_specs=out_specs, check_vma=False)
```

```python
import functools

import jax
import jax.numpy as jnp
from jax import lax
from jax.experimental import pallas as pl
from jax.experimental.pallas import tpu as pltpu
from jax.sharding import PartitionSpec as P

TILE_H = 8
TILE_W = 128
MESH = pl.DeviceIdType.MESH
BF = jnp.bfloat16
F32 = jnp.float32
ROOT_HALF = 0.7071067811865476
NORM_CONST = 0.3989422804014327


def dot(a, b):
    return lax.dot_general(a, b, (((1,), (0,)), ((), ())), preferred_element_type=F32)


def dot_t(a, b):
    return lax.dot_general(a, b, (((1,), (1,)), ((), ())), preferred_element_type=F32)


def gelu_parts(v):
    e = 0.5 * (1.0 + lax.erf(v * ROOT_HALF))
    return v * e, e + v * jnp.exp(-0.5 * v * v) * NORM_CONST


def coords():
    lon, filt = lax.axis_index("lon"), lax.axis_index("filt")
    y, x = filt // 4, filt % 4
    v = x // 2
    u = (x + v) % 2
    return lon, filt, u, v, y


def filt_of(u, v, y):
    return 4 * y + 2 * v + (u + v) % 2


def kernel(
    x_ref, c_ref, win_ref, wout_ref, tiles_ref,
    block_ref, state_ref, gout_ref, gin_ref,
    xr, cr, w1, w2, w3, w4, maskv, tedge, hal, hs, gps, edge, hedge, keep, s1, r1, s2, r2, s3, r3, sums,
    gacc, gx, gxr, gsum, gs, gr, gall, goth,
    hals_sem, halr_sem, send_sem, recv_sem, gxs_sem, gxr_sem, gs_sem, gr_sem, ga_sem, gar_sem, go_sem, gor_sem,
):
    lon, filt, u, v, y = coords()
    core = lon % 2
    chip = lon // 2
    lane256 = lax.broadcasted_iota(jnp.int32, (128, 256), 1)
    partners = ((lon, filt_of(1 - u, v, y)), (lon, filt_of(u, 1 - v, y)), (lon, filt_of(u, v, 1 - y)))
    mate = (chip * 2 + (1 - core), filt)
    far = ((lon + 15 + 2 * core) % 16, filt)

    def peer(d):
        z, yl = chip % 4, chip // 4
        z = (z + d % 4) % 4
        yl = (yl + d // 4) % 2
        return yl * 4 + z

    def opposite(d):
        return (4 - d % 4) % 4 + (d // 4) * 4

    barrier = pltpu.get_barrier_semaphore()
    for who in partners + (mate, far):
        pl.semaphore_signal(barrier, inc=1, device_id=who, device_id_type=MESH)
    for d in range(1, 8):
        pl.semaphore_signal(barrier, inc=1, device_id=(peer(d) * 2 + core, filt), device_id_type=MESH)

    def flag(tile_row, offset):
        return tiles_ref[tile_row, (2 * lon + 32 + offset) % 32].astype(F32)

    wide = lax.broadcasted_iota(jnp.int32, (1, 256), 1)
    for t in range(2):
        line = jnp.where(wide < 128, flag(t, 0), flag(t, 1))
        for r in range(8):
            maskv[8 * t + r] = line
    laneh = lax.broadcasted_iota(jnp.int32, (1, 128), 1)
    maskh = jnp.where(
        laneh < 64,
        jnp.where(laneh % 8 < 4, flag(0, -1), flag(0, 2)),
        jnp.where(laneh % 8 < 4, flag(1, -1), flag(1, 2)),
    )

    for ref in (xr, cr):
        ref[0] = jnp.zeros((256, 256), BF)
        ref[17] = jnp.zeros((256, 256), BF)
    for ref in (hs, gps):
        ref[0] = jnp.zeros((384, 256), BF)
        ref[17] = jnp.zeros((384, 256), BF)

    @pl.loop(0, 16)
    def _(b):
        part = pl.ds(pl.multiple_of(b * 16, 16), 16)
        m = maskv[...].astype(BF)
        xr[1:17, part, :] = jnp.swapaxes(x_ref[part], 0, 1) * m
        cr[1:17, part, :] = jnp.swapaxes(c_ref[part], 0, 1) * m

    lane_e = lax.broadcasted_iota(jnp.int32, (256, 128), 1)
    for a, ref in enumerate((xr, cr)):
        acc = jnp.zeros((256, 128), F32)
        for r in range(16):
            row = ref[r + 1].astype(F32)
            ends = jnp.where(lane_e < 64, row[:, 0:128], row[:, 128:256])
            acc = jnp.where(lane_e // 8 == r, pltpu.roll(ends, (8 * r + 2) % 128, 1), acc)
        acc = jnp.where(lane_e % 8 < 4, acc, pltpu.roll(acc, 4, 1))
        tedge[a] = acc.astype(BF)

    def halo_copy(i):
        return pltpu.make_async_remote_copy(
            src_ref=tedge, dst_ref=hal.at[i], send_sem=hals_sem.at[i], recv_sem=halr_sem.at[i],
            device_id=(mate, far)[i], device_id_type=MESH,
        )

    pl.semaphore_wait(barrier, 12)
    halo_copy(1).start()
    halo_copy(0).start()

    for k in range(9):
        w2[(k % 3) * 128 : (k % 3) * 128 + 128, (k // 3) * 256 : (k // 3) * 256 + 256] = wout_ref[8 - k]
    eye = (lax.broadcasted_iota(jnp.int32, (128, 128), 0) == lax.broadcasted_iota(jnp.int32, (128, 128), 1))
    flipped = dot_t(eye.astype(F32).astype(BF), win_ref[...].reshape(2304, 128))
    for k in range(9):
        w1[(k % 3) * 128 : (k % 3) * 128 + 128, (k // 3) * 256 : (k // 3) * 256 + 256] = flipped[
            :, k * 256 : k * 256 + 256
        ].astype(BF)
    place = lax.broadcasted_iota(jnp.int32, (256, 256), 0)
    chan = lax.broadcasted_iota(jnp.int32, (256, 256), 1)
    b1, b2, b3, low = place // 128, (place // 64) % 2, (place // 32) % 2, place % 32
    pick_a = (chan == 32 * filt_of((u + b1) % 2, (v + b3) % 2, (y + b2) % 2) + low).astype(F32).astype(BF)
    pick_b = (chan == 32 * filt_of((u + b3) % 2, (v + b1) % 2, (y + b2) % 2) + low).astype(F32).astype(BF)
    w3[...] = dot_t(pick_a, wout_ref[...].reshape(1152, 256)).astype(BF)
    w4[...] = dot(pick_b, jnp.concatenate([win_ref[8 - k] for k in range(9)], axis=1)).astype(BF)

    halo_copy(0).wait_recv()
    halo_copy(1).wait_recv()

    lane_h = lax.broadcasted_iota(jnp.int32, (384, 128), 1)

    def halo(w_ref, a):
        t = jnp.where(
            lane_e % 8 < 2,
            hal[1 - core, a].astype(F32),
            jnp.where(lane_e % 8 >= 6, hal[core, a].astype(F32), tedge[a].astype(F32)),
        ).astype(BF)
        total = dot(w_ref[:, 256:512], t)
        above = pltpu.roll(dot(w_ref[:, 0:256], t), 8, 1)
        below = pltpu.roll(dot(w_ref[:, 512:768], t), 120, 1)
        return total + jnp.where(lane_h < 8, 0.0, above) + jnp.where(lane_h >= 120, 0.0, below)

    def halo_mid(s):
        return pltpu.roll(s[0:128], 1, 1) + s[128:256] + pltpu.roll(s[256:384], 127, 1)

    sp = halo(w1, 0)
    sg = halo(w2, 1)
    edge[0] = sp[0:128]
    edge[1] = sp[256:384]
    edge[2] = sg[0:128]
    edge[3] = sg[256:384]
    act, slope = gelu_parts(halo_mid(sp))
    hedge[0] = act * maskh
    hedge[1] = halo_mid(sg) * slope * maskh

    def before(val, tile, row):
        moved = pltpu.roll(tile, 127 - 8 * row, 1)
        return jnp.where(lane256 == 0, jnp.concatenate([moved, moved], axis=1), pltpu.roll(val, 1, 1))

    def after(val, tile, row):
        moved = pltpu.roll(tile, 121 - 8 * row, 1)
        return jnp.where(lane256 == 255, jnp.concatenate([moved, moved], axis=1), pltpu.roll(val, 255, 1))

    def two_rows(ref, row, height):
        return jnp.concatenate(
            [ref[pl.ds(row, 3)].reshape(3 * height, 256), ref[pl.ds(row + 1, 3)].reshape(3 * height, 256)], axis=1
        )

    def first_stage(q):
        row0 = 2 * q
        zp = dot(w1[...], two_rows(xr, row0, 256))
        zg = dot(w2[...], two_rows(cr, row0, 256))
        for s in range(2):
            row = row0 + s
            a = zp[:, 256 * s : 256 * s + 256]
            b = zg[:, 256 * s : 256 * s + 256]
            pre = a[128:256] + before(a[0:128], edge[0], row) + after(a[256:384], edge[1], row)
            gh = b[128:256] + before(b[0:128], edge[2], row) + after(b[256:384], edge[3], row)
            mask = maskv[row]
            act, slope = gelu_parts(pre)
            for ref, val, tile in ((hs, act * mask, hedge[0]), (gps, gh * slope * mask, hedge[1])):
                ref[row + 1, 0:128] = before(val, tile, row).astype(BF)
                ref[row + 1, 128:256] = val.astype(BF)
                ref[row + 1, 256:384] = after(val, tile, row).astype(BF)

    bufs = ((s1, r1), (s2, r2), (s3, r3))
    order = ((0, 2, 1), (1, 2, 0))

    def hop(step, a, q):
        src, dst = bufs[step]
        return pltpu.make_async_remote_copy(
            src_ref=src.at[a, q], dst_ref=dst.at[a, q], send_sem=send_sem.at[step, a, q], recv_sem=recv_sem.at[step, a, q],
            device_id=partners[order[a][step]], device_id_type=MESH,
        )

    def second_stage(q):
        for a, (w_ref, ref) in enumerate(((w3, hs), (w4, gps))):
            res = dot(w_ref[...], two_rows(ref, 2 * q, 384))
            for s in range(2):
                part = res[:, 256 * s : 256 * s + 256]
                keep[a, q, s] = part[0:128]
                s1[a, q, s] = part[128:256].astype(BF)
            hop(0, a, q).start()

    def advance(step, q):
        left = (64, 32, 0)[step]
        for a in range(2):
            hop(step, a, q).wait_recv()
            for s in range(2):
                got = bufs[step][1][a, q, s].astype(F32)
                if step < 2:
                    total = keep[a, q, s, 0 : 2 * left] + got
                    keep[a, q, s, 0:left] = total[0:left]
                    bufs[step + 1][0][a, q, s] = total[left : 2 * left].astype(BF)
                else:
                    sums[a, 2 * q + s] = keep[a, q, s, 0:32] + got
            if step < 2:
                hop(step + 1, a, q).start()

    def progress(t):
        for step, lag in enumerate((3, 5, 7)):
            @pl.when((t >= lag) & (t < lag + 8))
            def _():
                advance(step, t - lag)

    @pl.loop(0, 9)
    def _(t):
        @pl.when(t < 8)
        def _():
            first_stage(t)

        @pl.when(t >= 1)
        def _():
            second_stage(t - 1)

        progress(t)

    def to_mate(g):
        return pltpu.make_async_remote_copy(
            src_ref=gx.at[g], dst_ref=gxr.at[g], send_sem=gxs_sem.at[g], recv_sem=gxr_sem.at[g],
            device_id=mate, device_id_type=MESH,
        )

    def scatter(g, d):
        return pltpu.make_async_remote_copy(
            src_ref=gs.at[g, peer(d)], dst_ref=gr.at[g, d], send_sem=gs_sem.at[g, d], recv_sem=gr_sem.at[g, d],
            device_id=(peer(d) * 2 + core, filt), device_id_type=MESH,
        )

    def spread(g, d):
        return pltpu.make_async_remote_copy(
            src_ref=gall.at[g, chip], dst_ref=gall.at[g, chip], send_sem=ga_sem.at[g, d], recv_sem=gar_sem.at[g, d],
            device_id=(peer(d) * 2 + core, filt), device_id_type=MESH,
        )

    def arrival(g, d):
        return pltpu.make_async_remote_copy(
            src_ref=gall.at[g, chip], dst_ref=gall.at[g, peer(opposite(d))], send_sem=ga_sem.at[g, d], recv_sem=gar_sem.at[g, d],
            device_id=(peer(d) * 2 + core, filt), device_id_type=MESH,
        )

    def across(g):
        return pltpu.make_async_remote_copy(
            src_ref=gall.at[g], dst_ref=goth.at[g], send_sem=go_sem.at[g], recv_sem=gor_sem.at[g],
            device_id=mate, device_id_type=MESH,
        )

    def four_rows(ref, row):
        return jnp.concatenate([ref[row + j] for j in range(4)], axis=1)

    def weight_round(g):
        gacc[...] = jnp.zeros((2, 6, 128, 128), F32)

        @pl.loop(0, 4)
        def _(b):
            res = dot_t(four_rows(hs, 4 * b + g), four_rows(cr, 4 * b + 1))
            for n in range(6):
                gacc[0, n] += res[(n // 2) * 128 : (n // 2) * 128 + 128, (n % 2) * 128 : (n % 2) * 128 + 128]
            res = dot_t(four_rows(xr, 4 * b + 1), four_rows(gps, 4 * b + g))
            for n in range(6):
                gacc[1, n] += res[(n // 3) * 128 : (n // 3) * 128 + 128, (n % 3) * 128 : (n % 3) * 128 + 128]

        gx[g] = gacc[1 - core].astype(BF)
        to_mate(g).start()

    def gather_mate(g):
        to_mate(g).wait_recv()
        for p in range(8):
            total = gacc[core, :, 16 * p : 16 * p + 16] + gxr[g, :, 16 * p : 16 * p + 16].astype(F32)
            gsum[g, p] = total
            gs[g, p] = total.astype(BF)
        for d in range(1, 8):
            scatter(g, d).start()

    def finish_piece(g):
        total = gsum[g, chip]
        for d in range(1, 8):
            scatter(g, d).wait_recv()
            total = total + gr[g, d].astype(F32)
        gall[g, chip] = total.astype(BF)
        for d in range(1, 8):
            spread(g, d).start()

    def swap_cores(g):
        for d in range(1, 8):
            arrival(g, d).wait_recv()
        across(g).start()

    @pl.loop(0, 3)
    def _(g):
        weight_round(g)

        @pl.when(g >= 1)
        def _():
            finish_piece(g - 1)

        progress(9 + 2 * g)
        gather_mate(g)
        progress(10 + 2 * g)

        @pl.when(g >= 1)
        def _():
            swap_cores(g - 1)

    mine = pl.ds(pl.multiple_of(filt * 32, 32), 32)
    for a, (ref, raw) in enumerate(((block_ref, x_ref), (state_ref, c_ref))):
        ref[...] = (raw[mine].astype(F32) + jnp.swapaxes(sums[a] * maskv[...], 0, 1)).astype(BF)

    finish_piece(2)
    swap_cores(2)
    for g in range(3):
        across(g).wait_recv()

    def put(first, second):
        for g in range(3):
            for p in range(8):
                rows = slice(16 * p, 16 * p + 16)
                for n in range(6):
                    gout_ref[3 * g + n // 2, rows, (n % 2) * 128 : (n % 2) * 128 + 128] = first[g, p, n]
                    half = (n // 3) * 128 + 16 * p
                    gin_ref[8 - (3 * g + n % 3), half : half + 16, :] = second[g, p, n]

    @pl.when(core == 0)
    def _():
        put(gall, goth)

    @pl.when(core == 1)
    def _():
        put(goth, gall)

    halo_copy(0).wait_send()
    halo_copy(1).wait_send()

    @pl.loop(0, 8)
    def _(q):
        for step in range(3):
            for a in range(2):
                hop(step, a, q).wait_send()

    @pl.loop(0, 3)
    def _(g):
        to_mate(g).wait_send()
        across(g).wait_send()
        for d in range(1, 8):
            scatter(g, d).wait_send()
            spread(g, d).wait_send()


def call_kernel(*args):
    vm = pltpu.VMEM
    dma = pltpu.SemaphoreType.DMA
    whole = pl.BlockSpec(memory_space=pltpu.VMEM)
    return pl.pallas_call(
        kernel,
        name="ocean_block",
        out_shape=(
            jax.ShapeDtypeStruct((32, 16, 256), BF),
            jax.ShapeDtypeStruct((32, 16, 256), BF),
            jax.ShapeDtypeStruct((9, 128, 256), BF),
            jax.ShapeDtypeStruct((9, 256, 128), BF),
        ),
        in_specs=[whole] * 4 + [pl.BlockSpec(memory_space=pltpu.SMEM)],
        out_specs=(whole,) * 4,
        scratch_shapes=[
            vm((18, 256, 256), BF), vm((18, 256, 256), BF),
            vm((384, 768), BF), vm((384, 768), BF), vm((256, 1152), BF), vm((256, 1152), BF),
            vm((16, 1, 256), F32), vm((2, 256, 128), BF), vm((2, 2, 256, 128), BF),
            vm((18, 384, 256), BF), vm((18, 384, 256), BF), vm((4, 128, 128), F32), vm((2, 128, 128), F32),
            vm((2, 8, 2, 128, 256), F32),
            vm((2, 8, 2, 128, 256), BF), vm((2, 8, 2, 128, 256), BF),
            vm((2, 8, 2, 64, 256), BF), vm((2, 8, 2, 64, 256), BF),
            vm((2, 8, 2, 32, 256), BF), vm((2, 8, 2, 32, 256), BF),
            vm((2, 16, 32, 256), F32),
            vm((2, 6, 128, 128), F32), vm((3, 6, 128, 128), BF), vm((3, 6, 128, 128), BF),
            vm((3, 8, 6, 16, 128), F32), vm((3, 8, 6, 16, 128), BF), vm((3, 8, 6, 16, 128), BF),
            vm((3, 8, 6, 16, 128), BF), vm((3, 8, 6, 16, 128), BF),
            dma((2,)), dma((2,)),
            dma((3, 2, 8)), dma((3, 2, 8)), dma((3,)), dma((3,)), dma((3, 8)), dma((3, 8)), dma((3, 8)), dma((3, 8)),
            dma((3,)), dma((3,)),
        ],
        compiler_params=pltpu.CompilerParams(
            collective_id=1, has_side_effects=True, vmem_limit_bytes=60 * 2**20
        ),
        cost_estimate=pl.CostEstimate(flops=14_500_000_000, bytes_accessed=10_000_000, transcendentals=1_000_000),
    )(*args)


def shards(ocean_state, cotangent, conv_in, conv_out, tile_mask):
    _, height, breadth = ocean_state.shape
    block_out, grad_state, grad_out, grad_in = call_kernel(ocean_state, cotangent, conv_in, conv_out, tile_mask)
    scale = 1.0 / (height * breadth * lax.axis_size("lon")) ** 0.5
    return (block_out, grad_state, grad_in.astype(F32) * scale, grad_out.astype(F32) * scale)


def solution(mesh):
    in_specs = (
        P(None, None, "lon"),
        P(None, None, "lon"),
        P(None, None, "filt"),
        P(None, "filt", None),
        P(),
    )
    out_specs = (
        P("filt", None, "lon"),
        P("filt", None, "lon"),
        P(None, None, "filt"),
        P(None, "filt", None),
    )
    return jax.shard_map(shards, mesh=mesh, in_specs=in_specs, out_specs=out_specs, check_vma=False)
```

```python
import functools

import jax
import jax.numpy as jnp
from jax import lax
from jax.experimental import pallas as pl
from jax.experimental.pallas import tpu as pltpu
from jax.sharding import PartitionSpec as P

TILE_H = 8
TILE_W = 128
MESH = pl.DeviceIdType.MESH
BF = jnp.bfloat16
F32 = jnp.float32
ROOT_HALF = 0.7071067811865476
NORM_CONST = 0.3989422804014327


def dot(a, b):
    return lax.dot_general(a, b, (((1,), (0,)), ((), ())), preferred_element_type=F32)


def dot_t(a, b):
    return lax.dot_general(a, b, (((1,), (1,)), ((), ())), preferred_element_type=F32)


def gelu_parts(v):
    e = 0.5 * (1.0 + lax.erf(v * ROOT_HALF))
    return v * e, e + v * jnp.exp(-0.5 * v * v) * NORM_CONST


def coords():
    lon, filt = lax.axis_index("lon"), lax.axis_index("filt")
    y, x = filt // 4, filt % 4
    v = x // 2
    u = (x + v) % 2
    return lon, filt, u, v, y


def filt_of(u, v, y):
    return 4 * y + 2 * v + (u + v) % 2


def kernel(
    x_hbm, c_hbm, win_hbm, wout_hbm, tiles_ref,
    block_ref, state_ref, gout_hbm, gin_hbm,
    x_ref, c_ref, win_ref, wout_ref, gout_ref, gin_ref, xr, cr, w1, w2, w3, w4, maskv, tedge, hal, hs, gps, edge, hedge, keep, s1, r1, s2, r2, s3, r3, sums,
    gacc, gxr, gsum, gs, gr, gy, gyr, gall, goth,
    in_sem, win_sem, out_sem, hals_sem, halr_sem, send_sem, recv_sem, gxs_sem, gxr_sem, gs_sem, gr_sem, gys_sem, gyr_sem, ga_sem, gar_sem, go_sem, gor_sem,
):
    lon, filt, u, v, y = coords()
    core = lon % 2
    chip = lon // 2
    lane256 = lax.broadcasted_iota(jnp.int32, (128, 256), 1)
    partners = ((lon, filt_of(1 - u, v, y)), (lon, filt_of(u, 1 - v, y)), (lon, filt_of(u, v, 1 - y)))
    mate = (chip * 2 + (1 - core), filt)
    far = ((lon + 15 + 2 * core) % 16, filt)

    z, yl = chip % 4, chip // 4

    def along(d):
        return ((yl * 4 + (z + d) % 4) * 2 + core, filt)

    ymate = (((1 - yl) * 4 + z) * 2 + core, filt)

    def take(a, n):
        part = pl.ds(pl.multiple_of(64 * n, 64), 64)
        return pltpu.make_async_copy((x_hbm, c_hbm)[a].at[part], (x_ref, c_ref)[a].at[part], in_sem.at[a, n])

    weights_in = (
        pltpu.make_async_copy(wout_hbm, wout_ref, win_sem.at[0]),
        pltpu.make_async_copy(win_hbm, win_ref, win_sem.at[1]),
    )
    for n in range(4):
        take(0, n).start()
        take(1, n).start()
    for copy in weights_in:
        copy.start()

    barrier = pltpu.get_barrier_semaphore()
    for who in partners + (mate, far, ymate):
        pl.semaphore_signal(barrier, inc=1, device_id=who, device_id_type=MESH)
    for d in range(1, 4):
        pl.semaphore_signal(barrier, inc=1, device_id=along(d), device_id_type=MESH)

    def flag(tile_row, offset):
        return tiles_ref[tile_row, (2 * lon + 32 + offset) % 32].astype(F32)

    wide = lax.broadcasted_iota(jnp.int32, (1, 256), 1)
    for t in range(2):
        line = jnp.where(wide < 128, flag(t, 0), flag(t, 1))
        for r in range(8):
            maskv[8 * t + r] = line
    laneh = lax.broadcasted_iota(jnp.int32, (1, 128), 1)
    maskh = jnp.where(
        laneh < 64,
        jnp.where(laneh % 8 < 4, flag(0, -1), flag(0, 2)),
        jnp.where(laneh % 8 < 4, flag(1, -1), flag(1, 2)),
    )

    for ref in (xr, cr):
        ref[0] = jnp.zeros((256, 256), BF)
        ref[17] = jnp.zeros((256, 256), BF)
    for ref in (hs, gps):
        ref[0] = jnp.zeros((384, 256), BF)
        ref[17] = jnp.zeros((384, 256), BF)

    @pl.loop(0, 16)
    def _(b):
        @pl.when(b % 4 == 0)
        def _():
            take(0, b // 4).wait()
            take(1, b // 4).wait()

        part = pl.ds(pl.multiple_of(b * 16, 16), 16)
        m = maskv[...].astype(BF)
        xr[1:17, part, :] = jnp.swapaxes(x_ref[part], 0, 1) * m
        cr[1:17, part, :] = jnp.swapaxes(c_ref[part], 0, 1) * m

    lane_e = lax.broadcasted_iota(jnp.int32, (256, 128), 1)
    for a, ref in enumerate((xr, cr)):
        acc = jnp.zeros((256, 128), F32)
        for r in range(16):
            row = ref[r + 1].astype(F32)
            ends = jnp.where(lane_e < 64, row[:, 0:128], row[:, 128:256])
            acc = jnp.where(lane_e // 8 == r, pltpu.roll(ends, (8 * r + 2) % 128, 1), acc)
        tedge[a] = jnp.where(lane_e % 8 < 4, acc, pltpu.roll(acc, 4, 1)).astype(BF)

    def halo_copy(i):
        return pltpu.make_async_remote_copy(
            src_ref=tedge, dst_ref=hal.at[i], send_sem=hals_sem.at[i], recv_sem=halr_sem.at[i],
            device_id=(mate, far)[i], device_id_type=MESH,
        )

    pl.semaphore_wait(barrier, 9)
    halo_copy(1).start()
    halo_copy(0).start()

    for copy in weights_in:
        copy.wait()
    for k in range(9):
        w2[(k % 3) * 128 : (k % 3) * 128 + 128, (k // 3) * 256 : (k // 3) * 256 + 256] = wout_ref[8 - k]
    eye = (lax.broadcasted_iota(jnp.int32, (128, 128), 0) == lax.broadcasted_iota(jnp.int32, (128, 128), 1))
    flipped = dot_t(eye.astype(F32).astype(BF), win_ref[...].reshape(2304, 128))
    for k in range(9):
        w1[(k % 3) * 128 : (k % 3) * 128 + 128, (k // 3) * 256 : (k // 3) * 256 + 256] = flipped[
            :, k * 256 : k * 256 + 256
        ].astype(BF)
    place = lax.broadcasted_iota(jnp.int32, (256, 256), 0)
    chan = lax.broadcasted_iota(jnp.int32, (256, 256), 1)
    b1, b2, b3, low = place // 128, (place // 64) % 2, (place // 32) % 2, place % 32
    pick_a = (chan == 32 * filt_of((u + b1) % 2, (v + b3) % 2, (y + b2) % 2) + low).astype(F32).astype(BF)
    pick_b = (chan == 32 * filt_of((u + b3) % 2, (v + b1) % 2, (y + b2) % 2) + low).astype(F32).astype(BF)
    w3[...] = dot_t(pick_a, wout_ref[...].reshape(1152, 256)).astype(BF)
    w4[...] = dot(pick_b, jnp.concatenate([win_ref[8 - k] for k in range(9)], axis=1)).astype(BF)

    halo_copy(0).wait_recv()
    halo_copy(1).wait_recv()

    lane_h = lax.broadcasted_iota(jnp.int32, (384, 128), 1)

    def halo(w_ref, a):
        t = jnp.where(
            lane_e % 8 < 2,
            hal[1 - core, a].astype(F32),
            jnp.where(lane_e % 8 >= 6, hal[core, a].astype(F32), tedge[a].astype(F32)),
        ).astype(BF)
        total = dot(w_ref[:, 256:512], t)
        above = pltpu.roll(dot(w_ref[:, 0:256], t), 8, 1)
        below = pltpu.roll(dot(w_ref[:, 512:768], t), 120, 1)
        return total + jnp.where(lane_h < 8, 0.0, above) + jnp.where(lane_h >= 120, 0.0, below)

    def halo_mid(s):
        return pltpu.roll(s[0:128], 1, 1) + s[128:256] + pltpu.roll(s[256:384], 127, 1)

    sp = halo(w1, 0)
    sg = halo(w2, 1)
    edge[0] = sp[0:128]
    edge[1] = sp[256:384]
    edge[2] = sg[0:128]
    edge[3] = sg[256:384]
    act, slope = gelu_parts(halo_mid(sp))
    hedge[0] = act * maskh
    hedge[1] = halo_mid(sg) * slope * maskh

    def before(val, tile, row):
        moved = pltpu.roll(tile, 127 - 8 * row, 1)
        return jnp.where(lane256 == 0, jnp.concatenate([moved, moved], axis=1), pltpu.roll(val, 1, 1))

    def after(val, tile, row):
        moved = pltpu.roll(tile, 121 - 8 * row, 1)
        return jnp.where(lane256 == 255, jnp.concatenate([moved, moved], axis=1), pltpu.roll(val, 255, 1))

    def two_rows(ref, row, height):
        return jnp.concatenate(
            [ref[pl.ds(row, 3)].reshape(3 * height, 256), ref[pl.ds(row + 1, 3)].reshape(3 * height, 256)], axis=1
        )

    def first_stage(q):
        row0 = 2 * q
        zp = dot(w1[...], two_rows(xr, row0, 256))
        zg = dot(w2[...], two_rows(cr, row0, 256))
        for s in range(2):
            row = row0 + s
            a = zp[:, 256 * s : 256 * s + 256]
            b = zg[:, 256 * s : 256 * s + 256]
            pre = a[128:256] + before(a[0:128], edge[0], row) + after(a[256:384], edge[1], row)
            gh = b[128:256] + before(b[0:128], edge[2], row) + after(b[256:384], edge[3], row)
            mask = maskv[row]
            act, slope = gelu_parts(pre)
            for ref, val, tile in ((hs, act * mask, hedge[0]), (gps, gh * slope * mask, hedge[1])):
                ref[row + 1, 0:128] = before(val, tile, row).astype(BF)
                ref[row + 1, 128:256] = val.astype(BF)
                ref[row + 1, 256:384] = after(val, tile, row).astype(BF)

    bufs = ((s1, r1), (s2, r2), (s3, r3))
    order = ((0, 2, 1), (1, 2, 0))

    def hop(step, a, q):
        src, dst = bufs[step]
        return pltpu.make_async_remote_copy(
            src_ref=src.at[a, q], dst_ref=dst.at[a, q], send_sem=send_sem.at[step, a, q], recv_sem=recv_sem.at[step, a, q],
            device_id=partners[order[a][step]], device_id_type=MESH,
        )

    def second_stage(q):
        for a, (w_ref, ref) in enumerate(((w3, hs), (w4, gps))):
            res = dot(w_ref[...], two_rows(ref, 2 * q, 384))
            for s in range(2):
                part = res[:, 256 * s : 256 * s + 256]
                keep[a, q, s] = part[0:128]
                s1[a, q, s] = part[128:256].astype(BF)
            hop(0, a, q).start()

    def advance(step, q):
        left = (64, 32, 0)[step]
        for a in range(2):
            hop(step, a, q).wait_recv()
            for s in range(2):
                got = bufs[step][1][a, q, s].astype(F32)
                if step < 2:
                    total = keep[a, q, s, 0 : 2 * left] + got
                    keep[a, q, s, 0:left] = total[0:left]
                    bufs[step + 1][0][a, q, s] = total[left : 2 * left].astype(BF)
                else:
                    sums[a, 2 * q + s] = keep[a, q, s, 0:32] + got
            if step < 2:
                hop(step + 1, a, q).start()

    def to_mate(g):
        return pltpu.make_async_remote_copy(
            src_ref=gacc.at[g, 1 - core], dst_ref=gxr.at[g], send_sem=gxs_sem.at[g], recv_sem=gxr_sem.at[g],
            device_id=mate, device_id_type=MESH,
        )

    def scatter(g, d):
        return pltpu.make_async_remote_copy(
            src_ref=gs.at[g, (z + d) % 4], dst_ref=gr.at[g, d], send_sem=gs_sem.at[g, d], recv_sem=gr_sem.at[g, d],
            device_id=along(d), device_id_type=MESH,
        )

    def to_ymate(g):
        return pltpu.make_async_remote_copy(
            src_ref=gy.at[g], dst_ref=gyr.at[g], send_sem=gys_sem.at[g], recv_sem=gyr_sem.at[g],
            device_id=ymate, device_id_type=MESH,
        )

    def spread(g, d):
        return pltpu.make_async_remote_copy(
            src_ref=gall.at[g, z], dst_ref=gall.at[g, z], send_sem=ga_sem.at[g, d], recv_sem=gar_sem.at[g, d],
            device_id=along(d), device_id_type=MESH,
        )

    def arrival(g, d):
        return pltpu.make_async_remote_copy(
            src_ref=gall.at[g, z], dst_ref=gall.at[g, (z + 4 - d) % 4], send_sem=ga_sem.at[g, d], recv_sem=gar_sem.at[g, d],
            device_id=along(d), device_id_type=MESH,
        )

    def across(g):
        return pltpu.make_async_remote_copy(
            src_ref=gall.at[g], dst_ref=goth.at[g], send_sem=go_sem.at[g], recv_sem=gor_sem.at[g],
            device_id=mate, device_id_type=MESH,
        )

    def four_rows(ref, row):
        return jnp.concatenate([ref[row + j] for j in range(4)], axis=1)

    def weight_out(g):
        gacc[g, 0] = jnp.zeros((6, 128, 128), F32)

        @pl.loop(0, 4)
        def _(b):
            res = dot_t(four_rows(hs, 4 * b + g), four_rows(cr, 4 * b + 1))
            for n in range(6):
                gacc[g, 0, n] += res[(n // 2) * 128 : (n // 2) * 128 + 128, (n % 2) * 128 : (n % 2) * 128 + 128]

    def weight_in(g):
        gacc[g, 1] = jnp.zeros((6, 128, 128), F32)

        @pl.loop(0, 4)
        def _(b):
            res = dot_t(four_rows(xr, 4 * b + 1), four_rows(gps, 4 * b + g))
            for n in range(6):
                gacc[g, 1, n] += res[(n // 3) * 128 : (n // 3) * 128 + 128, (n % 3) * 128 : (n % 3) * 128 + 128]

        to_mate(g).start()

    def gather_mate(g):
        to_mate(g).wait_recv()
        for p in range(4):
            rows = slice(32 * p, 32 * p + 32)
            total = gacc[g, core, :, rows] + gxr[g, :, rows]
            gsum[g, p] = total
            gs[g, p] = total.astype(BF)
        for d in range(1, 4):
            scatter(g, d).start()

    def finish_piece(g):
        total = gsum[g, z]
        for d in range(1, 4):
            scatter(g, d).wait_recv()
            total = total + gr[g, d].astype(F32)
        gy[g] = total.astype(BF)
        to_ymate(g).start()

    def finish_both(g):
        to_ymate(g).wait_recv()
        gall[g, z] = (gy[g].astype(F32) + gyr[g].astype(F32)).astype(BF)
        for d in range(1, 4):
            spread(g, d).start()

    def swap_cores(g):
        for d in range(1, 4):
            arrival(g, d).wait_recv()
        across(g).start()

    def put(g):
        across(g).wait_recv()

        def lay(first, second):
            @pl.loop(0, 4)
            def _(p):
                rows = pl.ds(pl.multiple_of(32 * p, 32), 32)
                for n in range(6):
                    gout_ref[3 * g + n // 2, rows, (n % 2) * 128 : (n % 2) * 128 + 128] = first[g, p, n]
                    half = pl.ds(pl.multiple_of((n // 3) * 128 + 32 * p, 32), 32)
                    gin_ref[8 - (3 * g + n % 3), half, :] = second[g, p, n]

        @pl.when(core == 0)
        def _():
            lay(gall, goth)

        @pl.when(core == 1)
        def _():
            lay(goth, gall)

        for copy in written(g):
            copy.start()

    def written(g):
        return (
            pltpu.make_async_copy(gout_ref.at[pl.ds(3 * g, 3)], gout_hbm.at[pl.ds(3 * g, 3)], out_sem.at[0, g]),
            pltpu.make_async_copy(gin_ref.at[pl.ds(6 - 3 * g, 3)], gin_hbm.at[pl.ds(6 - 3 * g, 3)], out_sem.at[1, g]),
        )

    @pl.loop(0, 13)
    def _(j):
        def span(first, count, action):
            @pl.when((j >= first) & (j < first + count))
            def _():
                action(j - first)

        @pl.when(j < 4)
        def _():
            @pl.loop(0, 2)
            def _(i):
                first_stage(2 * j + i)

        span(0, 8, second_stage)
        span(4, 3, weight_out)
        span(5, 3, gather_mate)
        span(4, 3, weight_in)
        span(2, 8, functools.partial(advance, 0))
        span(4, 8, functools.partial(advance, 1))
        span(5, 8, functools.partial(advance, 2))
        span(6, 3, finish_piece)
        span(7, 3, finish_both)
        span(9, 3, swap_cores)
        span(10, 2, put)

    mine = pl.ds(pl.multiple_of(filt * 32, 32), 32)
    for a, (ref, raw) in enumerate(((block_ref, x_ref), (state_ref, c_ref))):
        ref[...] = (raw[mine].astype(F32) + jnp.swapaxes(sums[a] * maskv[...], 0, 1)).astype(BF)
    put(2)
    for g in range(3):
        for copy in written(g):
            copy.wait()

    halo_copy(0).wait_send()
    halo_copy(1).wait_send()

    @pl.loop(0, 8)
    def _(q):
        for step in range(3):
            for a in range(2):
                hop(step, a, q).wait_send()

    @pl.loop(0, 3)
    def _(g):
        to_mate(g).wait_send()
        across(g).wait_send()
        to_ymate(g).wait_send()
        for d in range(1, 4):
            scatter(g, d).wait_send()
            spread(g, d).wait_send()


def call_kernel(*args):
    vm = pltpu.VMEM
    dma = pltpu.SemaphoreType.DMA
    whole = pl.BlockSpec(memory_space=pltpu.VMEM)
    return pl.pallas_call(
        kernel,
        name="ocean_block",
        out_shape=(
            jax.ShapeDtypeStruct((32, 16, 256), BF),
            jax.ShapeDtypeStruct((32, 16, 256), BF),
            jax.ShapeDtypeStruct((9, 128, 256), BF),
            jax.ShapeDtypeStruct((9, 256, 128), BF),
        ),
        in_specs=[pl.BlockSpec(memory_space=pl.ANY)] * 4 + [pl.BlockSpec(memory_space=pltpu.SMEM)],
        out_specs=(whole, whole, pl.BlockSpec(memory_space=pl.ANY), pl.BlockSpec(memory_space=pl.ANY)),
        scratch_shapes=[
            vm((256, 16, 256), BF), vm((256, 16, 256), BF), vm((9, 256, 128), BF), vm((9, 128, 256), BF),
            vm((9, 128, 256), BF), vm((9, 256, 128), BF),
            vm((18, 256, 256), BF), vm((18, 256, 256), BF),
            vm((384, 768), BF), vm((384, 768), BF), vm((256, 1152), BF), vm((256, 1152), BF),
            vm((16, 1, 256), F32), vm((2, 256, 128), BF), vm((2, 2, 256, 128), BF),
            vm((18, 384, 256), BF), vm((18, 384, 256), BF), vm((4, 128, 128), F32), vm((2, 128, 128), F32),
            vm((2, 8, 2, 128, 256), F32),
            vm((2, 8, 2, 128, 256), BF), vm((2, 8, 2, 128, 256), BF),
            vm((2, 8, 2, 64, 256), BF), vm((2, 8, 2, 64, 256), BF),
            vm((2, 8, 2, 32, 256), BF), vm((2, 8, 2, 32, 256), BF),
            vm((2, 16, 32, 256), F32),
            vm((3, 2, 6, 128, 128), F32), vm((3, 6, 128, 128), F32),
            vm((3, 4, 6, 32, 128), F32), vm((3, 4, 6, 32, 128), BF), vm((3, 4, 6, 32, 128), BF),
            vm((3, 6, 32, 128), BF), vm((3, 6, 32, 128), BF),
            vm((3, 4, 6, 32, 128), BF), vm((3, 4, 6, 32, 128), BF),
            dma((2, 4)), dma((2,)), dma((2, 3)), dma((2,)), dma((2,)),
            dma((3, 2, 8)), dma((3, 2, 8)), dma((3,)), dma((3,)), dma((3, 4)), dma((3, 4)), dma((3,)), dma((3,)),
            dma((3, 4)), dma((3, 4)), dma((3,)), dma((3,)),
        ],
        compiler_params=pltpu.CompilerParams(
            collective_id=1, has_side_effects=True, vmem_limit_bytes=60 * 2**20
        ),
        cost_estimate=pl.CostEstimate(flops=14_500_000_000, bytes_accessed=10_000_000, transcendentals=1_000_000),
    )(*args)


def finish_kernel(
    scale, block_in, state_in, gout_in, gin_in, block_out, state_out, gout_out, gin_out, gb, gf, hb, hf, bb, sb, sem,
):
    come = tuple(
        pltpu.make_async_copy(src, dst, sem.at[n])
        for n, (src, dst) in enumerate(((gout_in, gb), (gin_in, hb), (block_in, bb), (state_in, sb)))
    )
    go = tuple(
        pltpu.make_async_copy(src, dst, sem.at[4 + n])
        for n, (src, dst) in enumerate(((gf, gout_out), (hf, gin_out), (bb, block_out), (sb, state_out)))
    )
    for copy in come:
        copy.start()
    for i, (narrow, wide) in enumerate(((gb, gf), (hb, hf))):
        come[i].wait()
        wide[...] = narrow[...].astype(F32) * scale
        go[i].start()
    for i in (2, 3):
        come[i].wait()
        go[i].start()
    for copy in go:
        copy.wait()


def finish(scale, *args):
    anywhere = pl.BlockSpec(memory_space=pl.ANY)
    vm = pltpu.VMEM
    return pl.pallas_call(
        functools.partial(finish_kernel, scale),
        name="widen",
        out_shape=(
            jax.ShapeDtypeStruct((32, 16, 256), BF),
            jax.ShapeDtypeStruct((32, 16, 256), BF),
            jax.ShapeDtypeStruct((9, 128, 256), F32),
            jax.ShapeDtypeStruct((9, 256, 128), F32),
        ),
        in_specs=[anywhere] * 4,
        out_specs=(anywhere,) * 4,
        scratch_shapes=[
            vm((9, 128, 256), BF), vm((9, 128, 256), F32), vm((9, 256, 128), BF), vm((9, 256, 128), F32),
            vm((32, 16, 256), BF), vm((32, 16, 256), BF), pltpu.SemaphoreType.DMA((8,)),
        ],
        compiler_params=pltpu.CompilerParams(vmem_limit_bytes=62 * 2**20),
    )(*args)


def shards(ocean_state, cotangent, conv_in, conv_out, tile_mask):
    _, height, breadth = ocean_state.shape
    scale = 1.0 / (height * breadth * lax.axis_size("lon")) ** 0.5
    parts = call_kernel(ocean_state, cotangent, conv_in, conv_out, tile_mask)
    block_out, grad_state, grad_out, grad_in = finish(scale, *parts)
    return (block_out, grad_state, grad_in, grad_out)


def solution(mesh):
    in_specs = (
        P(None, None, "lon"),
        P(None, None, "lon"),
        P(None, None, "filt"),
        P(None, "filt", None),
        P(),
    )
    out_specs = (
        P("filt", None, "lon"),
        P("filt", None, "lon"),
        P(None, None, "filt"),
        P(None, "filt", None),
    )
    return jax.shard_map(shards, mesh=mesh, in_specs=in_specs, out_specs=out_specs, check_vma=False)
```

```python
import functools

import jax
import jax.numpy as jnp
from jax import lax
from jax.experimental import pallas as pl
from jax.experimental.pallas import tpu as pltpu
from jax.sharding import PartitionSpec as P

TILE_H = 8
TILE_W = 128
MESH = pl.DeviceIdType.MESH
BF = jnp.bfloat16
F32 = jnp.float32
ROOT_HALF = 0.7071067811865476
NORM_CONST = 0.3989422804014327


def dot(a, b):
    return lax.dot_general(a, b, (((1,), (0,)), ((), ())), preferred_element_type=F32)


def dot_t(a, b):
    return lax.dot_general(a, b, (((1,), (1,)), ((), ())), preferred_element_type=F32)


def gelu_parts(v):
    e = 0.5 * (1.0 + lax.erf(v * ROOT_HALF))
    return v * e, e + v * jnp.exp(-0.5 * v * v) * NORM_CONST


def coords():
    lon, filt = lax.axis_index("lon"), lax.axis_index("filt")
    y, x = filt // 4, filt % 4
    v = x // 2
    u = (x + v) % 2
    return lon, filt, u, v, y


def filt_of(u, v, y):
    return 4 * y + 2 * v + (u + v) % 2


def kernel(
    x_hbm, c_hbm, win_hbm, wout_hbm, tiles_ref,
    block_ref, state_ref, gout_hbm, gin_hbm,
    x_ref, c_ref, win_ref, wout_ref, gout_ref, gin_ref, xr, cr, w1, w2, w3, w4, maskv, choose, tacc, tedge, hal, hs, gps, edge, hedge, keep, s1, r1, s2, r2, s3, r3, sums,
    gacc, gxr, gsum, gs, gr, gy, gyr, gall, goth,
    in_sem, win_sem, out_sem, hals_sem, halr_sem, send_sem, recv_sem, gxs_sem, gxr_sem, gs_sem, gr_sem, gys_sem, gyr_sem, ga_sem, gar_sem, go_sem, gor_sem,
):
    lon, filt, u, v, y = coords()
    core = lon % 2
    chip = lon // 2
    lane256 = lax.broadcasted_iota(jnp.int32, (128, 256), 1)
    partners = ((lon, filt_of(1 - u, v, y)), (lon, filt_of(u, 1 - v, y)), (lon, filt_of(u, v, 1 - y)))
    mate = (chip * 2 + (1 - core), filt)
    far = ((lon + 15 + 2 * core) % 16, filt)

    z, yl = chip % 4, chip // 4

    def along(d):
        return ((yl * 4 + (z + d) % 4) * 2 + core, filt)

    ymate = (((1 - yl) * 4 + z) * 2 + core, filt)

    def take(a, n):
        part = pl.ds(pl.multiple_of(64 * n, 64), 64)
        return pltpu.make_async_copy((x_hbm, c_hbm)[a].at[part], (x_ref, c_ref)[a].at[part], in_sem.at[a, n])

    weights_in = (
        pltpu.make_async_copy(wout_hbm, wout_ref, win_sem.at[0]),
        pltpu.make_async_copy(win_hbm, win_ref, win_sem.at[1]),
    )
    for n in range(4):
        take(0, n).start()
        take(1, n).start()
    for copy in weights_in:
        copy.start()

    barrier = pltpu.get_barrier_semaphore()
    for who in partners + (mate, far, ymate):
        pl.semaphore_signal(barrier, inc=1, device_id=who, device_id_type=MESH)
    for d in range(1, 4):
        pl.semaphore_signal(barrier, inc=1, device_id=along(d), device_id_type=MESH)

    def flag(tile_row, offset):
        return tiles_ref[tile_row, (2 * lon + 32 + offset) % 32].astype(F32)

    wide = lax.broadcasted_iota(jnp.int32, (1, 256), 1)
    for t in range(2):
        line = jnp.where(wide < 128, flag(t, 0), flag(t, 1))
        for r in range(8):
            maskv[8 * t + r] = line
    laneh = lax.broadcasted_iota(jnp.int32, (1, 128), 1)
    maskh = jnp.where(
        laneh < 64,
        jnp.where(laneh % 8 < 4, flag(0, -1), flag(0, 2)),
        jnp.where(laneh % 8 < 4, flag(1, -1), flag(1, 2)),
    )

    for ref in (xr, cr):
        ref[0] = jnp.zeros((256, 256), BF)
        ref[17] = jnp.zeros((256, 256), BF)
    for ref in (hs, gps):
        ref[0] = jnp.zeros((384, 256), BF)
        ref[17] = jnp.zeros((384, 256), BF)

    spot = lax.broadcasted_iota(jnp.int32, (512, 128), 0)
    slot = lax.broadcasted_iota(jnp.int32, (512, 128), 1)

    @pl.loop(0, 4)
    def _(g):
        hit = (slot // 8 == 4 * g + spot // 128) & ((slot % 4 + 126) % 128 == spot % 128)
        choose[g] = hit.astype(F32).astype(BF)

    tacc[...] = jnp.zeros((2, 256, 128), F32)

    @pl.loop(0, 16)
    def _(b):
        @pl.when(b % 4 == 0)
        def _():
            take(0, b // 4).wait()
            take(1, b // 4).wait()

        part = pl.ds(pl.multiple_of(b * 16, 16), 16)
        m = maskv[...].astype(BF)
        xr[1:17, part, :] = jnp.swapaxes(x_ref[part], 0, 1) * m
        cr[1:17, part, :] = jnp.swapaxes(c_ref[part], 0, 1) * m

    lane_e = lax.broadcasted_iota(jnp.int32, (256, 128), 1)

    @pl.loop(0, 4)
    def _(g):
        for a, ref in enumerate((xr, cr)):
            ends = []
            for r in range(4):
                row = ref[4 * g + r + 1]
                ends.append(jnp.where(lane_e < 64, row[:, 0:128], row[:, 128:256]))
            tacc[a] += dot(jnp.concatenate(ends, axis=1), choose[g])

    tedge[...] = tacc[...].astype(BF)

    def halo_copy(i):
        return pltpu.make_async_remote_copy(
            src_ref=tedge, dst_ref=hal.at[i], send_sem=hals_sem.at[i], recv_sem=halr_sem.at[i],
            device_id=(mate, far)[i], device_id_type=MESH,
        )

    pl.semaphore_wait(barrier, 9)
    halo_copy(1).start()
    halo_copy(0).start()

    for copy in weights_in:
        copy.wait()
    for k in range(9):
        w2[(k % 3) * 128 : (k % 3) * 128 + 128, (k // 3) * 256 : (k // 3) * 256 + 256] = wout_ref[8 - k]
    eye = (lax.broadcasted_iota(jnp.int32, (128, 128), 0) == lax.broadcasted_iota(jnp.int32, (128, 128), 1))
    flipped = dot_t(eye.astype(F32).astype(BF), win_ref[...].reshape(2304, 128))
    for k in range(9):
        w1[(k % 3) * 128 : (k % 3) * 128 + 128, (k // 3) * 256 : (k // 3) * 256 + 256] = flipped[
            :, k * 256 : k * 256 + 256
        ].astype(BF)
    place = lax.broadcasted_iota(jnp.int32, (256, 256), 0)
    chan = lax.broadcasted_iota(jnp.int32, (256, 256), 1)
    b1, b2, b3, low = place // 128, (place // 64) % 2, (place // 32) % 2, place % 32
    pick_a = (chan == 32 * filt_of((u + b1) % 2, (v + b2) % 2, (y + b3) % 2) + low).astype(F32).astype(BF)
    pick_b = (chan == 32 * filt_of((u + b3) % 2, (v + b1) % 2, (y + b2) % 2) + low).astype(F32).astype(BF)
    w3[...] = dot_t(pick_a, wout_ref[...].reshape(1152, 256)).astype(BF)
    w4[...] = dot(pick_b, jnp.concatenate([win_ref[8 - k] for k in range(9)], axis=1)).astype(BF)

    halo_copy(0).wait_recv()
    halo_copy(1).wait_recv()

    lane_h = lax.broadcasted_iota(jnp.int32, (384, 128), 1)

    def halo(w_ref, a):
        t = jnp.where(
            lane_e % 8 < 2,
            hal[1 - core, a].astype(F32),
            jnp.where(lane_e % 8 >= 6, hal[core, a].astype(F32), tedge[a].astype(F32)),
        ).astype(BF)
        total = dot(w_ref[:, 256:512], t)
        above = pltpu.roll(dot(w_ref[:, 0:256], t), 8, 1)
        below = pltpu.roll(dot(w_ref[:, 512:768], t), 120, 1)
        return total + jnp.where(lane_h < 8, 0.0, above) + jnp.where(lane_h >= 120, 0.0, below)

    def halo_mid(s):
        return pltpu.roll(s[0:128], 1, 1) + s[128:256] + pltpu.roll(s[256:384], 127, 1)

    sp = halo(w1, 0)
    sg = halo(w2, 1)
    edge[0] = sp[0:128]
    edge[1] = sp[256:384]
    edge[2] = sg[0:128]
    edge[3] = sg[256:384]
    act, slope = gelu_parts(halo_mid(sp))
    hedge[0] = act * maskh
    hedge[1] = halo_mid(sg) * slope * maskh

    def before(val, tile, row):
        moved = pltpu.roll(tile, 127 - 8 * row, 1)
        return jnp.where(lane256 == 0, jnp.concatenate([moved, moved], axis=1), pltpu.roll(val, 1, 1))

    def after(val, tile, row):
        moved = pltpu.roll(tile, 121 - 8 * row, 1)
        return jnp.where(lane256 == 255, jnp.concatenate([moved, moved], axis=1), pltpu.roll(val, 255, 1))

    def two_rows(ref, row, height):
        return jnp.concatenate(
            [ref[pl.ds(row, 3)].reshape(3 * height, 256), ref[pl.ds(row + 1, 3)].reshape(3 * height, 256)], axis=1
        )

    def first_stage(q):
        row0 = 2 * q
        zp = dot(w1[...], two_rows(xr, row0, 256))
        zg = dot(w2[...], two_rows(cr, row0, 256))
        for s in range(2):
            row = row0 + s
            a = zp[:, 256 * s : 256 * s + 256]
            b = zg[:, 256 * s : 256 * s + 256]
            pre = a[128:256] + before(a[0:128], edge[0], row) + after(a[256:384], edge[1], row)
            gh = b[128:256] + before(b[0:128], edge[2], row) + after(b[256:384], edge[3], row)
            mask = maskv[row]
            act, slope = gelu_parts(pre)
            for ref, val, tile in ((hs, act * mask, hedge[0]), (gps, gh * slope * mask, hedge[1])):
                ref[row + 1, 0:128] = before(val, tile, row).astype(BF)
                ref[row + 1, 128:256] = val.astype(BF)
                ref[row + 1, 256:384] = after(val, tile, row).astype(BF)

    bufs = ((s1, r1), (s2, r2), (s3, r3))
    order = ((0, 1, 2), (1, 2, 0))

    def hop(step, a, q):
        src, dst = bufs[step]
        return pltpu.make_async_remote_copy(
            src_ref=src.at[a, q], dst_ref=dst.at[a, q], send_sem=send_sem.at[step, a, q], recv_sem=recv_sem.at[step, a, q],
            device_id=partners[order[a][step]], device_id_type=MESH,
        )

    def second_stage(q):
        for a, (w_ref, ref) in enumerate(((w3, hs), (w4, gps))):
            res = dot(w_ref[...], two_rows(ref, 2 * q, 384))
            for s in range(2):
                part = res[:, 256 * s : 256 * s + 256]
                keep[a, q, s] = part[0:128]
                s1[a, q, s] = part[128:256].astype(BF)
            hop(0, a, q).start()

    def advance(step, q):
        left = (64, 32, 0)[step]
        for a in range(2):
            hop(step, a, q).wait_recv()
            for s in range(2):
                got = bufs[step][1][a, q, s].astype(F32)
                if step < 2:
                    total = keep[a, q, s, 0 : 2 * left] + got
                    keep[a, q, s, 0:left] = total[0:left]
                    bufs[step + 1][0][a, q, s] = total[left : 2 * left].astype(BF)
                else:
                    sums[a, 2 * q + s] = keep[a, q, s, 0:32] + got
            if step < 2:
                hop(step + 1, a, q).start()

    def to_mate(g):
        return pltpu.make_async_remote_copy(
            src_ref=gacc.at[g, 1 - core], dst_ref=gxr.at[g], send_sem=gxs_sem.at[g], recv_sem=gxr_sem.at[g],
            device_id=mate, device_id_type=MESH,
        )

    def scatter(g, d):
        return pltpu.make_async_remote_copy(
            src_ref=gs.at[g, (z + d) % 4], dst_ref=gr.at[g, d], send_sem=gs_sem.at[g, d], recv_sem=gr_sem.at[g, d],
            device_id=along(d), device_id_type=MESH,
        )

    def to_ymate(g):
        return pltpu.make_async_remote_copy(
            src_ref=gy.at[g], dst_ref=gyr.at[g], send_sem=gys_sem.at[g], recv_sem=gyr_sem.at[g],
            device_id=ymate, device_id_type=MESH,
        )

    def spread(g, d):
        return pltpu.make_async_remote_copy(
            src_ref=gall.at[g, z], dst_ref=gall.at[g, z], send_sem=ga_sem.at[g, d], recv_sem=gar_sem.at[g, d],
            device_id=along(d), device_id_type=MESH,
        )

    def arrival(g, d):
        return pltpu.make_async_remote_copy(
            src_ref=gall.at[g, z], dst_ref=gall.at[g, (z + 4 - d) % 4], send_sem=ga_sem.at[g, d], recv_sem=gar_sem.at[g, d],
            device_id=along(d), device_id_type=MESH,
        )

    def across(g):
        return pltpu.make_async_remote_copy(
            src_ref=gall.at[g], dst_ref=goth.at[g], send_sem=go_sem.at[g], recv_sem=gor_sem.at[g],
            device_id=mate, device_id_type=MESH,
        )

    def four_rows(ref, row):
        return jnp.concatenate([ref[row + j] for j in range(4)], axis=1)

    def weight_out(g):
        gacc[g, 0] = jnp.zeros((6, 128, 128), F32)

        @pl.loop(0, 4)
        def _(b):
            res = dot_t(four_rows(hs, 4 * b + g), four_rows(cr, 4 * b + 1))
            for n in range(6):
                gacc[g, 0, n] += res[(n // 2) * 128 : (n // 2) * 128 + 128, (n % 2) * 128 : (n % 2) * 128 + 128]

    def weight_in(g):
        gacc[g, 1] = jnp.zeros((6, 128, 128), F32)

        @pl.loop(0, 4)
        def _(b):
            res = dot_t(four_rows(xr, 4 * b + 1), four_rows(gps, 4 * b + g))
            for n in range(6):
                gacc[g, 1, n] += res[(n // 3) * 128 : (n // 3) * 128 + 128, (n % 3) * 128 : (n % 3) * 128 + 128]

        to_mate(g).start()

    def gather_mate(g):
        to_mate(g).wait_recv()
        for p in range(4):
            rows = slice(32 * p, 32 * p + 32)
            total = gacc[g, core, :, rows] + gxr[g, :, rows]
            gsum[g, p] = total
            gs[g, p] = total.astype(BF)
        for d in range(1, 4):
            scatter(g, d).start()

    def finish_piece(g):
        total = gsum[g, z]
        for d in range(1, 4):
            scatter(g, d).wait_recv()
            total = total + gr[g, d].astype(F32)
        gy[g] = total.astype(BF)
        to_ymate(g).start()

    def finish_both(g):
        to_ymate(g).wait_recv()
        gall[g, z] = (gy[g].astype(F32) + gyr[g].astype(F32)).astype(BF)
        for d in range(1, 4):
            spread(g, d).start()

    def swap_cores(g):
        for d in range(1, 4):
            arrival(g, d).wait_recv()
        across(g).start()

    def put(g):
        across(g).wait_recv()

        def lay(first, second):
            @pl.loop(0, 4)
            def _(p):
                rows = pl.ds(pl.multiple_of(32 * p, 32), 32)
                for n in range(6):
                    gout_ref[3 * g + n // 2, rows, (n % 2) * 128 : (n % 2) * 128 + 128] = first[g, p, n]
                    half = pl.ds(pl.multiple_of((n // 3) * 128 + 32 * p, 32), 32)
                    gin_ref[8 - (3 * g + n % 3), half, :] = second[g, p, n]

        @pl.when(core == 0)
        def _():
            lay(gall, goth)

        @pl.when(core == 1)
        def _():
            lay(goth, gall)

        for copy in written(g):
            copy.start()

    def written(g):
        return (
            pltpu.make_async_copy(gout_ref.at[pl.ds(3 * g, 3)], gout_hbm.at[pl.ds(3 * g, 3)], out_sem.at[0, g]),
            pltpu.make_async_copy(gin_ref.at[pl.ds(6 - 3 * g, 3)], gin_hbm.at[pl.ds(6 - 3 * g, 3)], out_sem.at[1, g]),
        )

    @pl.loop(0, 13)
    def _(j):
        def span(first, count, action):
            @pl.when((j >= first) & (j < first + count))
            def _():
                action(j - first)

        @pl.when(j < 4)
        def _():
            @pl.loop(0, 2)
            def _(i):
                first_stage(2 * j + i)

        span(0, 8, second_stage)
        span(4, 3, weight_out)
        span(5, 3, gather_mate)
        span(4, 3, weight_in)
        span(2, 8, functools.partial(advance, 0))
        span(4, 8, functools.partial(advance, 1))
        span(5, 8, functools.partial(advance, 2))
        span(6, 3, finish_piece)
        span(7, 3, finish_both)
        span(9, 3, swap_cores)
        span(10, 2, put)

    mine = pl.ds(pl.multiple_of(filt * 32, 32), 32)
    for a, (ref, raw) in enumerate(((block_ref, x_ref), (state_ref, c_ref))):
        ref[...] = (raw[mine].astype(F32) + jnp.swapaxes(sums[a] * maskv[...], 0, 1)).astype(BF)
    put(2)
    for g in range(3):
        for copy in written(g):
            copy.wait()

    halo_copy(0).wait_send()
    halo_copy(1).wait_send()

    @pl.loop(0, 8)
    def _(q):
        for step in range(3):
            for a in range(2):
                hop(step, a, q).wait_send()

    @pl.loop(0, 3)
    def _(g):
        to_mate(g).wait_send()
        across(g).wait_send()
        to_ymate(g).wait_send()
        for d in range(1, 4):
            scatter(g, d).wait_send()
            spread(g, d).wait_send()


def call_kernel(*args):
    vm = pltpu.VMEM
    dma = pltpu.SemaphoreType.DMA
    whole = pl.BlockSpec(memory_space=pltpu.VMEM)
    return pl.pallas_call(
        kernel,
        name="ocean_block",
        out_shape=(
            jax.ShapeDtypeStruct((32, 16, 256), BF),
            jax.ShapeDtypeStruct((32, 16, 256), BF),
            jax.ShapeDtypeStruct((9, 128, 256), BF),
            jax.ShapeDtypeStruct((9, 256, 128), BF),
        ),
        in_specs=[pl.BlockSpec(memory_space=pl.ANY)] * 4 + [pl.BlockSpec(memory_space=pltpu.SMEM)],
        out_specs=(whole, whole, pl.BlockSpec(memory_space=pl.ANY), pl.BlockSpec(memory_space=pl.ANY)),
        scratch_shapes=[
            vm((256, 16, 256), BF), vm((256, 16, 256), BF), vm((9, 256, 128), BF), vm((9, 128, 256), BF),
            vm((9, 128, 256), BF), vm((9, 256, 128), BF),
            vm((18, 256, 256), BF), vm((18, 256, 256), BF),
            vm((384, 768), BF), vm((384, 768), BF), vm((256, 1152), BF), vm((256, 1152), BF),
            vm((16, 1, 256), F32), vm((4, 512, 128), BF), vm((2, 256, 128), F32), vm((2, 256, 128), BF), vm((2, 2, 256, 128), BF),
            vm((18, 384, 256), BF), vm((18, 384, 256), BF), vm((4, 128, 128), F32), vm((2, 128, 128), F32),
            vm((2, 8, 2, 128, 256), F32),
            vm((2, 8, 2, 128, 256), BF), vm((2, 8, 2, 128, 256), BF),
            vm((2, 8, 2, 64, 256), BF), vm((2, 8, 2, 64, 256), BF),
            vm((2, 8, 2, 32, 256), BF), vm((2, 8, 2, 32, 256), BF),
            vm((2, 16, 32, 256), F32),
            vm((3, 2, 6, 128, 128), F32), vm((3, 6, 128, 128), F32),
            vm((3, 4, 6, 32, 128), F32), vm((3, 4, 6, 32, 128), BF), vm((3, 4, 6, 32, 128), BF),
            vm((3, 6, 32, 128), BF), vm((3, 6, 32, 128), BF),
            vm((3, 4, 6, 32, 128), BF), vm((3, 4, 6, 32, 128), BF),
            dma((2, 4)), dma((2,)), dma((2, 3)), dma((2,)), dma((2,)),
            dma((3, 2, 8)), dma((3, 2, 8)), dma((3,)), dma((3,)), dma((3, 4)), dma((3, 4)), dma((3,)), dma((3,)),
            dma((3, 4)), dma((3, 4)), dma((3,)), dma((3,)),
        ],
        compiler_params=pltpu.CompilerParams(
            collective_id=1, has_side_effects=True, vmem_limit_bytes=60 * 2**20
        ),
        cost_estimate=pl.CostEstimate(flops=14_500_000_000, bytes_accessed=10_000_000, transcendentals=1_000_000),
    )(*args)


def finish_kernel(
    scale, block_in, state_in, gout_in, gin_in, block_out, state_out, gout_out, gin_out, gb, gf, hb, hf, bb, sb, sem,
):
    pieces = [(gout_in, gb, gf, gout_out, n) for n in range(3)] + [(gin_in, hb, hf, gin_out, n) for n in range(3)]
    thirds = [pl.ds(3 * n, 3) for n in range(3)]
    come = [
        pltpu.make_async_copy(src.at[thirds[n]], narrow.at[thirds[n]], sem.at[0, i])
        for i, (src, narrow, _, _, n) in enumerate(pieces)
    ]
    go = [
        pltpu.make_async_copy(wide.at[thirds[n]], dst.at[thirds[n]], sem.at[1, i])
        for i, (_, _, wide, dst, n) in enumerate(pieces)
    ]
    for i, (src, held, dst) in enumerate(((block_in, bb, block_out), (state_in, sb, state_out))):
        come.append(pltpu.make_async_copy(src, held, sem.at[0, 6 + i]))
        go.append(pltpu.make_async_copy(held, dst, sem.at[1, 6 + i]))
    for copy in come:
        copy.start()
    for i, (_, narrow, wide, _, n) in enumerate(pieces):
        come[i].wait()
        wide[thirds[n]] = narrow[thirds[n]].astype(F32) * scale
        go[i].start()
    for i in (6, 7):
        come[i].wait()
        go[i].start()
    for copy in go:
        copy.wait()


def finish(scale, *args):
    anywhere = pl.BlockSpec(memory_space=pl.ANY)
    vm = pltpu.VMEM
    return pl.pallas_call(
        functools.partial(finish_kernel, scale),
        name="widen",
        out_shape=(
            jax.ShapeDtypeStruct((32, 16, 256), BF),
            jax.ShapeDtypeStruct((32, 16, 256), BF),
            jax.ShapeDtypeStruct((9, 128, 256), F32),
            jax.ShapeDtypeStruct((9, 256, 128), F32),
        ),
        in_specs=[anywhere] * 4,
        out_specs=(anywhere,) * 4,
        scratch_shapes=[
            vm((9, 128, 256), BF), vm((9, 128, 256), F32), vm((9, 256, 128), BF), vm((9, 256, 128), F32),
            vm((32, 16, 256), BF), vm((32, 16, 256), BF), pltpu.SemaphoreType.DMA((2, 8)),
        ],
        compiler_params=pltpu.CompilerParams(vmem_limit_bytes=62 * 2**20),
    )(*args)


def shards(ocean_state, cotangent, conv_in, conv_out, tile_mask):
    _, height, breadth = ocean_state.shape
    scale = 1.0 / (height * breadth * lax.axis_size("lon")) ** 0.5
    parts = call_kernel(ocean_state, cotangent, conv_in, conv_out, tile_mask)
    block_out, grad_state, grad_out, grad_in = finish(scale, *parts)
    return (block_out, grad_state, grad_in, grad_out)


def solution(mesh):
    in_specs = (
        P(None, None, "lon"),
        P(None, None, "lon"),
        P(None, None, "filt"),
        P(None, "filt", None),
        P(),
    )
    out_specs = (
        P("filt", None, "lon"),
        P("filt", None, "lon"),
        P(None, None, "filt"),
        P(None, "filt", None),
    )
    return jax.shard_map(shards, mesh=mesh, in_specs=in_specs, out_specs=out_specs, check_vma=False)
```

```python
import functools

import jax
import jax.numpy as jnp
from jax import lax
from jax.experimental import pallas as pl
from jax.experimental.pallas import tpu as pltpu
from jax.sharding import PartitionSpec as P

TILE_H = 8
TILE_W = 128
MESH = pl.DeviceIdType.MESH
BF = jnp.bfloat16
F32 = jnp.float32
ROOT_HALF = 0.7071067811865476
NORM_CONST = 0.3989422804014327


def dot(a, b):
    return lax.dot_general(a, b, (((1,), (0,)), ((), ())), preferred_element_type=F32)


def dot_t(a, b):
    return lax.dot_general(a, b, (((1,), (1,)), ((), ())), preferred_element_type=F32)


def gelu_parts(v):
    e = 0.5 * (1.0 + lax.erf(v * ROOT_HALF))
    return v * e, e + v * jnp.exp(-0.5 * v * v) * NORM_CONST


def coords():
    lon, filt = lax.axis_index("lon"), lax.axis_index("filt")
    y, x = filt // 4, filt % 4
    v = x // 2
    u = (x + v) % 2
    return lon, filt, u, v, y


def filt_of(u, v, y):
    return 4 * y + 2 * v + (u + v) % 2


def kernel(
    x_hbm, c_hbm, win_hbm, wout_hbm, tiles_ref,
    block_ref, state_ref, gout_hbm, gin_hbm,
    x_ref, c_ref, win_ref, wout_ref, gout_ref, gin_ref, xr, cr, w1, w2, w3, w4, maskv, choose, tacc, tedge, hal, hs, gps, edge, hedge, keep, s1, r1, s2, r2, s3, r3, sums,
    gacc, gxr, gsum, gs, gr, gy, gyr, gall, goth,
    in_sem, win_sem, out_sem, hals_sem, halr_sem, send_sem, recv_sem, gxs_sem, gxr_sem, gs_sem, gr_sem, gys_sem, gyr_sem, ga_sem, gar_sem, go_sem, gor_sem,
):
    lon, filt, u, v, y = coords()
    core = lon % 2
    chip = lon // 2
    lane256 = lax.broadcasted_iota(jnp.int32, (128, 256), 1)
    partners = ((lon, filt_of(1 - u, v, y)), (lon, filt_of(u, 1 - v, y)), (lon, filt_of(u, v, 1 - y)))
    mate = (chip * 2 + (1 - core), filt)
    far = ((lon + 15 + 2 * core) % 16, filt)

    z, yl = chip % 4, chip // 4

    def along(d):
        return ((yl * 4 + (z + d) % 4) * 2 + core, filt)

    ymate = (((1 - yl) * 4 + z) * 2 + core, filt)

    def take(a, n):
        part = pl.ds(pl.multiple_of(64 * n, 64), 64)
        return pltpu.make_async_copy((x_hbm, c_hbm)[a].at[part], (x_ref, c_ref)[a].at[part], in_sem.at[a, n])

    weights_in = (
        pltpu.make_async_copy(wout_hbm, wout_ref, win_sem.at[0]),
        pltpu.make_async_copy(win_hbm, win_ref, win_sem.at[1]),
    )
    for n in range(4):
        take(0, n).start()
        take(1, n).start()
    for copy in weights_in:
        copy.start()

    barrier = pltpu.get_barrier_semaphore()
    for who in partners + (mate, far, ymate):
        pl.semaphore_signal(barrier, inc=1, device_id=who, device_id_type=MESH)
    for d in range(1, 4):
        pl.semaphore_signal(barrier, inc=1, device_id=along(d), device_id_type=MESH)

    def flag(tile_row, offset):
        return tiles_ref[tile_row, (2 * lon + 32 + offset) % 32].astype(F32)

    wide = lax.broadcasted_iota(jnp.int32, (1, 256), 1)
    for t in range(2):
        line = jnp.where(wide < 128, flag(t, 0), flag(t, 1))
        for r in range(8):
            maskv[8 * t + r] = line
    laneh = lax.broadcasted_iota(jnp.int32, (1, 128), 1)
    maskh = jnp.where(
        laneh < 64,
        jnp.where(laneh % 8 < 4, flag(0, -1), flag(0, 2)),
        jnp.where(laneh % 8 < 4, flag(1, -1), flag(1, 2)),
    )

    for ref in (xr, cr):
        ref[0] = jnp.zeros((256, 256), BF)
        ref[17] = jnp.zeros((256, 256), BF)
    for ref in (hs, gps):
        ref[0] = jnp.zeros((384, 256), BF)
        ref[17] = jnp.zeros((384, 256), BF)

    spot = lax.broadcasted_iota(jnp.int32, (512, 128), 0)
    slot = lax.broadcasted_iota(jnp.int32, (512, 128), 1)

    @pl.loop(0, 4)
    def _(g):
        hit = (slot // 8 == 4 * g + spot // 128) & ((slot % 4 + 126) % 128 == spot % 128)
        choose[g] = hit.astype(F32).astype(BF)

    tacc[...] = jnp.zeros((2, 256, 128), F32)

    @pl.loop(0, 16)
    def _(b):
        @pl.when(b % 4 == 0)
        def _():
            take(0, b // 4).wait()
            take(1, b // 4).wait()

        part = pl.ds(pl.multiple_of(b * 16, 16), 16)
        m = maskv[...].astype(BF)
        xr[1:17, part, :] = jnp.swapaxes(x_ref[part], 0, 1) * m
        cr[1:17, part, :] = jnp.swapaxes(c_ref[part], 0, 1) * m

    lane_e = lax.broadcasted_iota(jnp.int32, (256, 128), 1)

    @pl.loop(0, 4)
    def _(g):
        for a, ref in enumerate((xr, cr)):
            ends = []
            for r in range(4):
                row = ref[4 * g + r + 1]
                ends.append(jnp.where(lane_e < 64, row[:, 0:128], row[:, 128:256]))
            tacc[a] += dot(jnp.concatenate(ends, axis=1), choose[g])

    tedge[...] = tacc[...].astype(BF)

    def halo_copy(i):
        return pltpu.make_async_remote_copy(
            src_ref=tedge, dst_ref=hal.at[i], send_sem=hals_sem.at[i], recv_sem=halr_sem.at[i],
            device_id=(mate, far)[i], device_id_type=MESH,
        )

    pl.semaphore_wait(barrier, 9)
    halo_copy(1).start()
    halo_copy(0).start()

    for copy in weights_in:
        copy.wait()
    for k in range(9):
        w2[(k % 3) * 128 : (k % 3) * 128 + 128, (k // 3) * 256 : (k // 3) * 256 + 256] = wout_ref[8 - k]
    eye = (lax.broadcasted_iota(jnp.int32, (128, 128), 0) == lax.broadcasted_iota(jnp.int32, (128, 128), 1))
    flipped = dot_t(eye.astype(F32).astype(BF), win_ref[...].reshape(2304, 128))
    for k in range(9):
        w1[(k % 3) * 128 : (k % 3) * 128 + 128, (k // 3) * 256 : (k // 3) * 256 + 256] = flipped[
            :, k * 256 : k * 256 + 256
        ].astype(BF)
    place = lax.broadcasted_iota(jnp.int32, (256, 256), 0)
    chan = lax.broadcasted_iota(jnp.int32, (256, 256), 1)
    b1, b2, b3, low = place // 128, (place // 64) % 2, (place // 32) % 2, place % 32
    pick_a = (chan == 32 * filt_of((u + b1) % 2, (v + b2) % 2, (y + b3) % 2) + low).astype(F32).astype(BF)
    pick_b = (chan == 32 * filt_of((u + b3) % 2, (v + b1) % 2, (y + b2) % 2) + low).astype(F32).astype(BF)
    w3[...] = dot_t(pick_a, wout_ref[...].reshape(1152, 256)).astype(BF)
    w4[...] = dot(pick_b, jnp.concatenate([win_ref[8 - k] for k in range(9)], axis=1)).astype(BF)

    halo_copy(0).wait_recv()
    halo_copy(1).wait_recv()

    lane_h = lax.broadcasted_iota(jnp.int32, (384, 128), 1)

    def halo(w_ref, a):
        t = jnp.where(
            lane_e % 8 < 2,
            hal[1 - core, a].astype(F32),
            jnp.where(lane_e % 8 >= 6, hal[core, a].astype(F32), tedge[a].astype(F32)),
        ).astype(BF)
        total = dot(w_ref[:, 256:512], t)
        above = pltpu.roll(dot(w_ref[:, 0:256], t), 8, 1)
        below = pltpu.roll(dot(w_ref[:, 512:768], t), 120, 1)
        return total + jnp.where(lane_h < 8, 0.0, above) + jnp.where(lane_h >= 120, 0.0, below)

    def halo_mid(s):
        return pltpu.roll(s[0:128], 1, 1) + s[128:256] + pltpu.roll(s[256:384], 127, 1)

    sp = halo(w1, 0)
    sg = halo(w2, 1)
    edge[0] = sp[0:128]
    edge[1] = sp[256:384]
    edge[2] = sg[0:128]
    edge[3] = sg[256:384]
    act, slope = gelu_parts(halo_mid(sp))
    hedge[0] = act * maskh
    hedge[1] = halo_mid(sg) * slope * maskh

    def before(val, tile, row):
        moved = pltpu.roll(tile, 127 - 8 * row, 1)
        return jnp.where(lane256 == 0, jnp.concatenate([moved, moved], axis=1), pltpu.roll(val, 1, 1))

    def after(val, tile, row):
        moved = pltpu.roll(tile, 121 - 8 * row, 1)
        return jnp.where(lane256 == 255, jnp.concatenate([moved, moved], axis=1), pltpu.roll(val, 255, 1))

    def two_rows(ref, row, height):
        return jnp.concatenate(
            [ref[pl.ds(row, 3)].reshape(3 * height, 256), ref[pl.ds(row + 1, 3)].reshape(3 * height, 256)], axis=1
        )

    def first_stage(q):
        row0 = 2 * q
        zp = dot(w1[...], two_rows(xr, row0, 256))
        zg = dot(w2[...], two_rows(cr, row0, 256))
        for s in range(2):
            row = row0 + s
            a = zp[:, 256 * s : 256 * s + 256]
            b = zg[:, 256 * s : 256 * s + 256]
            pre = a[128:256] + before(a[0:128], edge[0], row) + after(a[256:384], edge[1], row)
            gh = b[128:256] + before(b[0:128], edge[2], row) + after(b[256:384], edge[3], row)
            mask = maskv[row]
            act, slope = gelu_parts(pre)
            for ref, val, tile in ((hs, act * mask, hedge[0]), (gps, gh * slope * mask, hedge[1])):
                ref[row + 1, 0:128] = before(val, tile, row).astype(BF)
                ref[row + 1, 128:256] = val.astype(BF)
                ref[row + 1, 256:384] = after(val, tile, row).astype(BF)

    bufs = ((s1, r1), (s2, r2), (s3, r3))
    order = ((0, 1, 2), (1, 2, 0))

    def hop(step, a, q):
        src, dst = bufs[step]
        return pltpu.make_async_remote_copy(
            src_ref=src.at[a, q], dst_ref=dst.at[a, q], send_sem=send_sem.at[step, a, q], recv_sem=recv_sem.at[step, a, q],
            device_id=partners[order[a][step]], device_id_type=MESH,
        )

    def second_stage(q):
        for a, (w_ref, ref) in enumerate(((w3, hs), (w4, gps))):
            res = dot(w_ref[...], two_rows(ref, 2 * q, 384))
            for s in range(2):
                part = res[:, 256 * s : 256 * s + 256]
                keep[a, q, s] = part[0:128]
                s1[a, q, s] = part[128:256].astype(BF)
            hop(0, a, q).start()

    def advance(step, q):
        left = (64, 32, 0)[step]
        for a in range(2):
            hop(step, a, q).wait_recv()
            for s in range(2):
                got = bufs[step][1][a, q, s].astype(F32)
                if step < 2:
                    total = keep[a, q, s, 0 : 2 * left] + got
                    keep[a, q, s, 0:left] = total[0:left]
                    bufs[step + 1][0][a, q, s] = total[left : 2 * left].astype(BF)
                else:
                    sums[a, 2 * q + s] = keep[a, q, s, 0:32] + got
            if step < 2:
                hop(step + 1, a, q).start()

    def to_mate(g):
        return pltpu.make_async_remote_copy(
            src_ref=gacc.at[g, 1 - core], dst_ref=gxr.at[g], send_sem=gxs_sem.at[g], recv_sem=gxr_sem.at[g],
            device_id=mate, device_id_type=MESH,
        )

    def scatter(g, d):
        return pltpu.make_async_remote_copy(
            src_ref=gs.at[g, (z + d) % 4], dst_ref=gr.at[g, d], send_sem=gs_sem.at[g, d], recv_sem=gr_sem.at[g, d],
            device_id=along(d), device_id_type=MESH,
        )

    def to_ymate(g):
        return pltpu.make_async_remote_copy(
            src_ref=gy.at[g], dst_ref=gyr.at[g], send_sem=gys_sem.at[g], recv_sem=gyr_sem.at[g],
            device_id=ymate, device_id_type=MESH,
        )

    def spread(g, d):
        return pltpu.make_async_remote_copy(
            src_ref=gall.at[g, z], dst_ref=gall.at[g, z], send_sem=ga_sem.at[g, d], recv_sem=gar_sem.at[g, d],
            device_id=along(d), device_id_type=MESH,
        )

    def arrival(g, d):
        return pltpu.make_async_remote_copy(
            src_ref=gall.at[g, z], dst_ref=gall.at[g, (z + 4 - d) % 4], send_sem=ga_sem.at[g, d], recv_sem=gar_sem.at[g, d],
            device_id=along(d), device_id_type=MESH,
        )

    def across(g):
        return pltpu.make_async_remote_copy(
            src_ref=gall.at[g], dst_ref=goth.at[g], send_sem=go_sem.at[g], recv_sem=gor_sem.at[g],
            device_id=mate, device_id_type=MESH,
        )

    def four_rows(ref, row):
        return jnp.concatenate([ref[row + j] for j in range(4)], axis=1)

    def weight_round(g):
        gacc[g] = jnp.zeros((2, 6, 128, 128), F32)

        @pl.loop(0, 4)
        def _(b):
            res = dot_t(four_rows(hs, 4 * b + g), four_rows(cr, 4 * b + 1))
            other = dot_t(four_rows(xr, 4 * b + 1), four_rows(gps, 4 * b + g))
            for n in range(6):
                gacc[g, 0, n] += res[(n // 2) * 128 : (n // 2) * 128 + 128, (n % 2) * 128 : (n % 2) * 128 + 128]
                gacc[g, 1, n] += other[(n // 3) * 128 : (n // 3) * 128 + 128, (n % 3) * 128 : (n % 3) * 128 + 128]

        to_mate(g).start()

    def gather_mate(g):
        to_mate(g).wait_recv()
        for p in range(4):
            rows = slice(32 * p, 32 * p + 32)
            total = gacc[g, core, :, rows] + gxr[g, :, rows]
            gsum[g, p] = total
            gs[g, p] = total.astype(BF)
        for d in range(1, 4):
            scatter(g, d).start()

    def finish_piece(g):
        total = gsum[g, z]
        for d in range(1, 4):
            scatter(g, d).wait_recv()
            total = total + gr[g, d].astype(F32)
        gy[g] = total.astype(BF)
        to_ymate(g).start()

    def finish_both(g):
        to_ymate(g).wait_recv()
        gall[g, z] = (gy[g].astype(F32) + gyr[g].astype(F32)).astype(BF)
        for d in range(1, 4):
            spread(g, d).start()

    def swap_cores(g):
        for d in range(1, 4):
            arrival(g, d).wait_recv()
        across(g).start()

    def put(g):
        across(g).wait_recv()

        def lay(first, second):
            @pl.loop(0, 4)
            def _(p):
                rows = pl.ds(pl.multiple_of(32 * p, 32), 32)
                for n in range(6):
                    gout_ref[3 * g + n // 2, rows, (n % 2) * 128 : (n % 2) * 128 + 128] = first[g, p, n]
                    half = pl.ds(pl.multiple_of((n // 3) * 128 + 32 * p, 32), 32)
                    gin_ref[8 - (3 * g + n % 3), half, :] = second[g, p, n]

        @pl.when(core == 0)
        def _():
            lay(gall, goth)

        @pl.when(core == 1)
        def _():
            lay(goth, gall)

        for copy in written(g):
            copy.start()

    def written(g):
        return (
            pltpu.make_async_copy(gout_ref.at[pl.ds(3 * g, 3)], gout_hbm.at[pl.ds(3 * g, 3)], out_sem.at[0, g]),
            pltpu.make_async_copy(gin_ref.at[pl.ds(6 - 3 * g, 3)], gin_hbm.at[pl.ds(6 - 3 * g, 3)], out_sem.at[1, g]),
        )

    @pl.loop(0, 13)
    def _(j):
        def span(first, count, action):
            @pl.when((j >= first) & (j < first + count))
            def _():
                action(j - first)

        @pl.when(j < 4)
        def _():
            @pl.loop(0, 2)
            def _(i):
                first_stage(2 * j + i)

        span(0, 8, second_stage)
        span(4, 3, weight_round)
        span(5, 3, gather_mate)
        span(2, 8, functools.partial(advance, 0))
        span(4, 8, functools.partial(advance, 1))
        span(5, 8, functools.partial(advance, 2))
        span(6, 3, finish_piece)
        span(7, 3, finish_both)
        span(9, 3, swap_cores)
        span(10, 2, put)

    mine = pl.ds(pl.multiple_of(filt * 32, 32), 32)
    for a, (ref, raw) in enumerate(((block_ref, x_ref), (state_ref, c_ref))):
        ref[...] = (raw[mine].astype(F32) + jnp.swapaxes(sums[a] * maskv[...], 0, 1)).astype(BF)
    put(2)
    for g in range(3):
        for copy in written(g):
            copy.wait()

    halo_copy(0).wait_send()
    halo_copy(1).wait_send()

    @pl.loop(0, 8)
    def _(q):
        for step in range(3):
            for a in range(2):
                hop(step, a, q).wait_send()

    @pl.loop(0, 3)
    def _(g):
        to_mate(g).wait_send()
        across(g).wait_send()
        to_ymate(g).wait_send()
        for d in range(1, 4):
            scatter(g, d).wait_send()
            spread(g, d).wait_send()


def call_kernel(*args):
    vm = pltpu.VMEM
    dma = pltpu.SemaphoreType.DMA
    whole = pl.BlockSpec(memory_space=pltpu.VMEM)
    return pl.pallas_call(
        kernel,
        name="ocean_block",
        out_shape=(
            jax.ShapeDtypeStruct((32, 16, 256), BF),
            jax.ShapeDtypeStruct((32, 16, 256), BF),
            jax.ShapeDtypeStruct((9, 128, 256), BF),
            jax.ShapeDtypeStruct((9, 256, 128), BF),
        ),
        in_specs=[pl.BlockSpec(memory_space=pl.ANY)] * 4 + [pl.BlockSpec(memory_space=pltpu.SMEM)],
        out_specs=(whole, whole, pl.BlockSpec(memory_space=pl.ANY), pl.BlockSpec(memory_space=pl.ANY)),
        scratch_shapes=[
            vm((256, 16, 256), BF), vm((256, 16, 256), BF), vm((9, 256, 128), BF), vm((9, 128, 256), BF),
            vm((9, 128, 256), BF), vm((9, 256, 128), BF),
            vm((18, 256, 256), BF), vm((18, 256, 256), BF),
            vm((384, 768), BF), vm((384, 768), BF), vm((256, 1152), BF), vm((256, 1152), BF),
            vm((16, 1, 256), F32), vm((4, 512, 128), BF), vm((2, 256, 128), F32), vm((2, 256, 128), BF), vm((2, 2, 256, 128), BF),
            vm((18, 384, 256), BF), vm((18, 384, 256), BF), vm((4, 128, 128), F32), vm((2, 128, 128), F32),
            vm((2, 8, 2, 128, 256), F32),
            vm((2, 8, 2, 128, 256), BF), vm((2, 8, 2, 128, 256), BF),
            vm((2, 8, 2, 64, 256), BF), vm((2, 8, 2, 64, 256), BF),
            vm((2, 8, 2, 32, 256), BF), vm((2, 8, 2, 32, 256), BF),
            vm((2, 16, 32, 256), F32),
            vm((3, 2, 6, 128, 128), F32), vm((3, 6, 128, 128), F32),
            vm((3, 4, 6, 32, 128), F32), vm((3, 4, 6, 32, 128), BF), vm((3, 4, 6, 32, 128), BF),
            vm((3, 6, 32, 128), BF), vm((3, 6, 32, 128), BF),
            vm((3, 4, 6, 32, 128), BF), vm((3, 4, 6, 32, 128), BF),
            dma((2, 4)), dma((2,)), dma((2, 3)), dma((2,)), dma((2,)),
            dma((3, 2, 8)), dma((3, 2, 8)), dma((3,)), dma((3,)), dma((3, 4)), dma((3, 4)), dma((3,)), dma((3,)),
            dma((3, 4)), dma((3, 4)), dma((3,)), dma((3,)),
        ],
        compiler_params=pltpu.CompilerParams(
            collective_id=1, has_side_effects=True, vmem_limit_bytes=60 * 2**20
        ),
        cost_estimate=pl.CostEstimate(flops=14_500_000_000, bytes_accessed=10_000_000, transcendentals=1_000_000),
    )(*args)


def finish_kernel(
    scale, block_in, state_in, gout_in, gin_in, block_out, state_out, gout_out, gin_out, gb, gf, hb, hf, bb, sb, sem,
):
    pieces = [(gout_in, gb, gf, gout_out, n) for n in range(3)] + [(gin_in, hb, hf, gin_out, n) for n in range(3)]
    thirds = [pl.ds(3 * n, 3) for n in range(3)]
    come = [
        pltpu.make_async_copy(src.at[thirds[n]], narrow.at[thirds[n]], sem.at[0, i])
        for i, (src, narrow, _, _, n) in enumerate(pieces)
    ]
    go = [
        pltpu.make_async_copy(wide.at[thirds[n]], dst.at[thirds[n]], sem.at[1, i])
        for i, (_, _, wide, dst, n) in enumerate(pieces)
    ]
    for i, (src, held, dst) in enumerate(((block_in, bb, block_out), (state_in, sb, state_out))):
        come.append(pltpu.make_async_copy(src, held, sem.at[0, 6 + i]))
        go.append(pltpu.make_async_copy(held, dst, sem.at[1, 6 + i]))
    for copy in come:
        copy.start()
    for i, (_, narrow, wide, _, n) in enumerate(pieces):
        come[i].wait()
        wide[thirds[n]] = narrow[thirds[n]].astype(F32) * scale
        go[i].start()
    for i in (6, 7):
        come[i].wait()
        go[i].start()
    for copy in go:
        copy.wait()


def finish(scale, *args):
    anywhere = pl.BlockSpec(memory_space=pl.ANY)
    vm = pltpu.VMEM
    return pl.pallas_call(
        functools.partial(finish_kernel, scale),
        name="widen",
        out_shape=(
            jax.ShapeDtypeStruct((32, 16, 256), BF),
            jax.ShapeDtypeStruct((32, 16, 256), BF),
            jax.ShapeDtypeStruct((9, 128, 256), F32),
            jax.ShapeDtypeStruct((9, 256, 128), F32),
        ),
        in_specs=[anywhere] * 4,
        out_specs=(anywhere,) * 4,
        scratch_shapes=[
            vm((9, 128, 256), BF), vm((9, 128, 256), F32), vm((9, 256, 128), BF), vm((9, 256, 128), F32),
            vm((32, 16, 256), BF), vm((32, 16, 256), BF), pltpu.SemaphoreType.DMA((2, 8)),
        ],
        compiler_params=pltpu.CompilerParams(vmem_limit_bytes=62 * 2**20),
    )(*args)


def shards(ocean_state, cotangent, conv_in, conv_out, tile_mask):
    _, height, breadth = ocean_state.shape
    scale = 1.0 / (height * breadth * lax.axis_size("lon")) ** 0.5
    parts = call_kernel(ocean_state, cotangent, conv_in, conv_out, tile_mask)
    block_out, grad_state, grad_out, grad_in = finish(scale, *parts)
    return (block_out, grad_state, grad_in, grad_out)


def solution(mesh):
    in_specs = (
        P(None, None, "lon"),
        P(None, None, "lon"),
        P(None, None, "filt"),
        P(None, "filt", None),
        P(),
    )
    out_specs = (
        P("filt", None, "lon"),
        P("filt", None, "lon"),
        P(None, None, "filt"),
        P(None, "filt", None),
    )
    return jax.shard_map(shards, mesh=mesh, in_specs=in_specs, out_specs=out_specs, check_vma=False)
```

```python
import functools

import jax
import jax.numpy as jnp
from jax import lax
from jax.experimental import pallas as pl
from jax.experimental.pallas import tpu as pltpu
from jax.sharding import PartitionSpec as P

TILE_H = 8
TILE_W = 128
MESH = pl.DeviceIdType.MESH
BF = jnp.bfloat16
F32 = jnp.float32
ROOT_HALF = 0.7071067811865476
NORM_CONST = 0.3989422804014327


def dot(a, b):
    return lax.dot_general(a, b, (((1,), (0,)), ((), ())), preferred_element_type=F32)


def dot_t(a, b):
    return lax.dot_general(a, b, (((1,), (1,)), ((), ())), preferred_element_type=F32)


def gelu_parts(v):
    e = 0.5 * (1.0 + lax.erf(v * ROOT_HALF))
    return v * e, e + v * jnp.exp(-0.5 * v * v) * NORM_CONST


def coords():
    lon, filt = lax.axis_index("lon"), lax.axis_index("filt")
    y, x = filt // 4, filt % 4
    v = x // 2
    u = (x + v) % 2
    return lon, filt, u, v, y


def filt_of(u, v, y):
    return 4 * y + 2 * v + (u + v) % 2


def kernel(
    x_hbm, c_hbm, win_hbm, wout_hbm, tiles_ref,
    block_ref, state_ref, gout_hbm, gin_hbm,
    x_ref, c_ref, win_ref, wout_ref, gout_ref, gin_ref, xr, cr, w1, w2, w3, w4, maskv, choose, tacc, tedge, hal, hs, gps, edge, hedge, keep, s1, r1, s2, r2, s3, r3, sums,
    gacc, gxr, gsum, gs, gr, gy, gyr, gall, goth,
    in_sem, win_sem, out_sem, hals_sem, halr_sem, send_sem, recv_sem, gxs_sem, gxr_sem, gs_sem, gr_sem, gys_sem, gyr_sem, ga_sem, gar_sem, go_sem, gor_sem,
):
    lon, filt, u, v, y = coords()
    core = lon % 2
    chip = lon // 2
    lane256 = lax.broadcasted_iota(jnp.int32, (128, 256), 1)
    partners = ((lon, filt_of(1 - u, v, y)), (lon, filt_of(u, 1 - v, y)), (lon, filt_of(u, v, 1 - y)))
    mate = (chip * 2 + (1 - core), filt)
    far = ((lon + 15 + 2 * core) % 16, filt)

    z, yl = chip % 4, chip // 4

    def along(d):
        return ((yl * 4 + (z + d) % 4) * 2 + core, filt)

    ymate = (((1 - yl) * 4 + z) * 2 + core, filt)

    def take(a, n):
        part = pl.ds(pl.multiple_of(64 * n, 64), 64)
        return pltpu.make_async_copy((x_hbm, c_hbm)[a].at[part], (x_ref, c_ref)[a].at[part], in_sem.at[a, n])

    weights_in = (
        pltpu.make_async_copy(wout_hbm, wout_ref, win_sem.at[0]),
        pltpu.make_async_copy(win_hbm, win_ref, win_sem.at[1]),
    )
    for n in range(4):
        take(0, n).start()
        take(1, n).start()
    for copy in weights_in:
        copy.start()

    barrier = pltpu.get_barrier_semaphore()
    for who in partners + (mate, far, ymate):
        pl.semaphore_signal(barrier, inc=1, device_id=who, device_id_type=MESH)
    for d in range(1, 4):
        pl.semaphore_signal(barrier, inc=1, device_id=along(d), device_id_type=MESH)

    def flag(tile_row, offset):
        return tiles_ref[tile_row, (2 * lon + 32 + offset) % 32].astype(F32)

    wide = lax.broadcasted_iota(jnp.int32, (1, 256), 1)
    for t in range(2):
        line = jnp.where(wide < 128, flag(t, 0), flag(t, 1))
        for r in range(8):
            maskv[8 * t + r] = line
    laneh = lax.broadcasted_iota(jnp.int32, (1, 128), 1)
    maskh = jnp.where(
        laneh < 64,
        jnp.where(laneh % 8 < 4, flag(0, -1), flag(0, 2)),
        jnp.where(laneh % 8 < 4, flag(1, -1), flag(1, 2)),
    )

    for ref in (xr, cr):
        ref[0] = jnp.zeros((256, 256), BF)
        ref[17] = jnp.zeros((256, 256), BF)
    for ref in (hs, gps):
        ref[0] = jnp.zeros((384, 256), BF)
        ref[17] = jnp.zeros((384, 256), BF)

    spot = lax.broadcasted_iota(jnp.int32, (512, 128), 0)
    slot = lax.broadcasted_iota(jnp.int32, (512, 128), 1)

    @pl.loop(0, 4)
    def _(g):
        hit = (slot // 8 == 4 * g + spot // 128) & ((slot % 4 + 126) % 128 == spot % 128)
        choose[g] = hit.astype(F32).astype(BF)

    tacc[...] = jnp.zeros((2, 256, 128), F32)

    @pl.loop(0, 16)
    def _(b):
        @pl.when(b % 4 == 0)
        def _():
            take(0, b // 4).wait()
            take(1, b // 4).wait()

        part = pl.ds(pl.multiple_of(b * 16, 16), 16)
        m = maskv[...].astype(BF)
        xr[1:17, part, :] = jnp.swapaxes(x_ref[part], 0, 1) * m
        cr[1:17, part, :] = jnp.swapaxes(c_ref[part], 0, 1) * m

    lane_e = lax.broadcasted_iota(jnp.int32, (256, 128), 1)

    @pl.loop(0, 4)
    def _(g):
        for a, ref in enumerate((xr, cr)):
            ends = []
            for r in range(4):
                row = ref[4 * g + r + 1]
                ends.append(jnp.where(lane_e < 64, row[:, 0:128], row[:, 128:256]))
            tacc[a] += dot(jnp.concatenate(ends, axis=1), choose[g])

    tedge[...] = tacc[...].astype(BF)

    def halo_copy(i):
        return pltpu.make_async_remote_copy(
            src_ref=tedge, dst_ref=hal.at[i], send_sem=hals_sem.at[i], recv_sem=halr_sem.at[i],
            device_id=(mate, far)[i], device_id_type=MESH,
        )

    pl.semaphore_wait(barrier, 9)
    halo_copy(1).start()
    halo_copy(0).start()

    for copy in weights_in:
        copy.wait()
    for k in range(9):
        w2[(k % 3) * 128 : (k % 3) * 128 + 128, (k // 3) * 256 : (k // 3) * 256 + 256] = wout_ref[8 - k]
    eye = (lax.broadcasted_iota(jnp.int32, (128, 128), 0) == lax.broadcasted_iota(jnp.int32, (128, 128), 1))
    flipped = dot_t(eye.astype(F32).astype(BF), win_ref[...].reshape(2304, 128))
    for k in range(9):
        w1[(k % 3) * 128 : (k % 3) * 128 + 128, (k // 3) * 256 : (k // 3) * 256 + 256] = flipped[
            :, k * 256 : k * 256 + 256
        ].astype(BF)
    place = lax.broadcasted_iota(jnp.int32, (256, 256), 0)
    chan = lax.broadcasted_iota(jnp.int32, (256, 256), 1)
    b1, b2, b3, low = place // 128, (place // 64) % 2, (place // 32) % 2, place % 32
    pick_a = (chan == 32 * filt_of((u + b1) % 2, (v + b2) % 2, (y + b3) % 2) + low).astype(F32).astype(BF)
    pick_b = (chan == 32 * filt_of((u + b3) % 2, (v + b1) % 2, (y + b2) % 2) + low).astype(F32).astype(BF)
    w3[...] = dot_t(pick_a, wout_ref[...].reshape(1152, 256)).astype(BF)
    w4[...] = dot(pick_b, jnp.concatenate([win_ref[8 - k] for k in range(9)], axis=1)).astype(BF)

    halo_copy(0).wait_recv()
    halo_copy(1).wait_recv()

    lane_h = lax.broadcasted_iota(jnp.int32, (384, 128), 1)

    def halo(w_ref, a):
        t = jnp.where(
            lane_e % 8 < 2,
            hal[1 - core, a].astype(F32),
            jnp.where(lane_e % 8 >= 6, hal[core, a].astype(F32), tedge[a].astype(F32)),
        ).astype(BF)
        total = dot(w_ref[:, 256:512], t)
        above = pltpu.roll(dot(w_ref[:, 0:256], t), 8, 1)
        below = pltpu.roll(dot(w_ref[:, 512:768], t), 120, 1)
        return total + jnp.where(lane_h < 8, 0.0, above) + jnp.where(lane_h >= 120, 0.0, below)

    def halo_mid(s):
        return pltpu.roll(s[0:128], 1, 1) + s[128:256] + pltpu.roll(s[256:384], 127, 1)

    sp = halo(w1, 0)
    sg = halo(w2, 1)
    edge[0] = sp[0:128]
    edge[1] = sp[256:384]
    edge[2] = sg[0:128]
    edge[3] = sg[256:384]
    act, slope = gelu_parts(halo_mid(sp))
    hedge[0] = act * maskh
    hedge[1] = halo_mid(sg) * slope * maskh

    def before(val, tile, row):
        moved = pltpu.roll(tile, 127 - 8 * row, 1)
        return jnp.where(lane256 == 0, jnp.concatenate([moved, moved], axis=1), pltpu.roll(val, 1, 1))

    def after(val, tile, row):
        moved = pltpu.roll(tile, 121 - 8 * row, 1)
        return jnp.where(lane256 == 255, jnp.concatenate([moved, moved], axis=1), pltpu.roll(val, 255, 1))

    def two_rows(ref, row, height):
        return jnp.concatenate(
            [ref[pl.ds(row, 3)].reshape(3 * height, 256), ref[pl.ds(row + 1, 3)].reshape(3 * height, 256)], axis=1
        )

    def first_stage(q):
        row0 = 2 * q
        zp = dot(w1[...], two_rows(xr, row0, 256))
        zg = dot(w2[...], two_rows(cr, row0, 256))
        for s in range(2):
            row = row0 + s
            a = zp[:, 256 * s : 256 * s + 256]
            b = zg[:, 256 * s : 256 * s + 256]
            pre = a[128:256] + before(a[0:128], edge[0], row) + after(a[256:384], edge[1], row)
            gh = b[128:256] + before(b[0:128], edge[2], row) + after(b[256:384], edge[3], row)
            mask = maskv[row]
            act, slope = gelu_parts(pre)
            for ref, val, tile in ((hs, act * mask, hedge[0]), (gps, gh * slope * mask, hedge[1])):
                ref[row + 1, 0:128] = before(val, tile, row).astype(BF)
                ref[row + 1, 128:256] = val.astype(BF)
                ref[row + 1, 256:384] = after(val, tile, row).astype(BF)

    bufs = ((s1, r1), (s2, r2), (s3, r3))
    order = ((0, 1, 2), (1, 2, 0))

    def hop(step, a, q):
        src, dst = bufs[step]
        return pltpu.make_async_remote_copy(
            src_ref=src.at[a, q], dst_ref=dst.at[a, q], send_sem=send_sem.at[step, a, q], recv_sem=recv_sem.at[step, a, q],
            device_id=partners[order[a][step]], device_id_type=MESH,
        )

    def second_stage(q):
        for a, (w_ref, ref) in enumerate(((w3, hs), (w4, gps))):
            res = dot(w_ref[...], two_rows(ref, 2 * q, 384))
            for s in range(2):
                part = res[:, 256 * s : 256 * s + 256]
                keep[a, q, s] = part[0:128]
                s1[a, q, s] = part[128:256].astype(BF)
            hop(0, a, q).start()

    def advance(step, q):
        left = (64, 32, 0)[step]
        for a in range(2):
            hop(step, a, q).wait_recv()
            for s in range(2):
                got = bufs[step][1][a, q, s].astype(F32)
                if step < 2:
                    total = keep[a, q, s, 0 : 2 * left] + got
                    keep[a, q, s, 0:left] = total[0:left]
                    bufs[step + 1][0][a, q, s] = total[left : 2 * left].astype(BF)
                else:
                    sums[a, 2 * q + s] = keep[a, q, s, 0:32] + got
            if step < 2:
                hop(step + 1, a, q).start()

    def to_mate(g):
        return pltpu.make_async_remote_copy(
            src_ref=gacc.at[g, 1 - core], dst_ref=gxr.at[g], send_sem=gxs_sem.at[g], recv_sem=gxr_sem.at[g],
            device_id=mate, device_id_type=MESH,
        )

    def scatter(g, d):
        return pltpu.make_async_remote_copy(
            src_ref=gs.at[g, (z + d) % 4], dst_ref=gr.at[g, d], send_sem=gs_sem.at[g, d], recv_sem=gr_sem.at[g, d],
            device_id=along(d), device_id_type=MESH,
        )

    def to_ymate(g):
        return pltpu.make_async_remote_copy(
            src_ref=gy.at[g], dst_ref=gyr.at[g], send_sem=gys_sem.at[g], recv_sem=gyr_sem.at[g],
            device_id=ymate, device_id_type=MESH,
        )

    def spread(g, d):
        return pltpu.make_async_remote_copy(
            src_ref=gall.at[g, z], dst_ref=gall.at[g, z], send_sem=ga_sem.at[g, d], recv_sem=gar_sem.at[g, d],
            device_id=along(d), device_id_type=MESH,
        )

    def arrival(g, d):
        return pltpu.make_async_remote_copy(
            src_ref=gall.at[g, z], dst_ref=gall.at[g, (z + 4 - d) % 4], send_sem=ga_sem.at[g, d], recv_sem=gar_sem.at[g, d],
            device_id=along(d), device_id_type=MESH,
        )

    def across(g):
        return pltpu.make_async_remote_copy(
            src_ref=gall.at[g], dst_ref=goth.at[g], send_sem=go_sem.at[g], recv_sem=gor_sem.at[g],
            device_id=mate, device_id_type=MESH,
        )

    def four_rows(ref, row):
        return jnp.concatenate([ref[row + j] for j in range(4)], axis=1)

    def weight_out(g):
        gacc[g, 0] = jnp.zeros((6, 128, 128), F32)

        @pl.loop(0, 4)
        def _(b):
            res = dot_t(four_rows(hs, 4 * b + g), four_rows(cr, 4 * b + 1))
            for n in range(6):
                gacc[g, 0, n] += res[(n // 2) * 128 : (n // 2) * 128 + 128, (n % 2) * 128 : (n % 2) * 128 + 128]

    def weight_in(g):
        gacc[g, 1] = jnp.zeros((6, 128, 128), F32)

        @pl.loop(0, 4)
        def _(b):
            res = dot_t(four_rows(xr, 4 * b + 1), four_rows(gps, 4 * b + g))
            for n in range(6):
                gacc[g, 1, n] += res[(n // 3) * 128 : (n // 3) * 128 + 128, (n % 3) * 128 : (n % 3) * 128 + 128]

        to_mate(g).start()

    def gather_mate(g):
        to_mate(g).wait_recv()
        for p in range(4):
            rows = slice(32 * p, 32 * p + 32)
            total = gacc[g, core, :, rows] + gxr[g, :, rows]
            gsum[g, p] = total
            gs[g, p] = total.astype(BF)
        for d in range(1, 4):
            scatter(g, d).start()

    def finish_piece(g):
        total = gsum[g, z]
        for d in range(1, 4):
            scatter(g, d).wait_recv()
            total = total + gr[g, d].astype(F32)
        gy[g] = total.astype(BF)
        to_ymate(g).start()

    def finish_both(g):
        to_ymate(g).wait_recv()
        gall[g, z] = (gy[g].astype(F32) + gyr[g].astype(F32)).astype(BF)
        for d in range(1, 4):
            spread(g, d).start()

    def swap_cores(g):
        for d in range(1, 4):
            arrival(g, d).wait_recv()
        across(g).start()

    def put(g):
        across(g).wait_recv()

        def lay(first, second):
            @pl.loop(0, 4)
            def _(p):
                rows = pl.ds(pl.multiple_of(32 * p, 32), 32)
                for n in range(6):
                    gout_ref[3 * g + n // 2, rows, (n % 2) * 128 : (n % 2) * 128 + 128] = first[g, p, n]
                    half = pl.ds(pl.multiple_of((n // 3) * 128 + 32 * p, 32), 32)
                    gin_ref[8 - (3 * g + n % 3), half, :] = second[g, p, n]

        @pl.when(core == 0)
        def _():
            lay(gall, goth)

        @pl.when(core == 1)
        def _():
            lay(goth, gall)

        for copy in written(g):
            copy.start()

    def written(g):
        return (
            pltpu.make_async_copy(gout_ref.at[pl.ds(3 * g, 3)], gout_hbm.at[pl.ds(3 * g, 3)], out_sem.at[0, g]),
            pltpu.make_async_copy(gin_ref.at[pl.ds(6 - 3 * g, 3)], gin_hbm.at[pl.ds(6 - 3 * g, 3)], out_sem.at[1, g]),
        )

    @pl.loop(0, 13)
    def _(j):
        def span(first, count, action):
            @pl.when((j >= first) & (j < first + count))
            def _():
                action(j - first)

        @pl.when(j < 4)
        def _():
            @pl.loop(0, 2)
            def _(i):
                first_stage(2 * j + i)

        span(0, 8, second_stage)
        span(4, 3, weight_out)
        span(2, 8, functools.partial(advance, 0))
        span(5, 3, gather_mate)
        span(4, 3, weight_in)
        span(4, 8, functools.partial(advance, 1))
        span(5, 8, functools.partial(advance, 2))
        span(6, 3, finish_piece)
        span(7, 3, finish_both)
        span(9, 3, swap_cores)
        span(10, 2, put)

    mine = pl.ds(pl.multiple_of(filt * 32, 32), 32)
    for a, (ref, raw) in enumerate(((block_ref, x_ref), (state_ref, c_ref))):
        ref[...] = (raw[mine].astype(F32) + jnp.swapaxes(sums[a] * maskv[...], 0, 1)).astype(BF)
    put(2)
    for g in range(3):
        for copy in written(g):
            copy.wait()

    halo_copy(0).wait_send()
    halo_copy(1).wait_send()

    @pl.loop(0, 8)
    def _(q):
        for step in range(3):
            for a in range(2):
                hop(step, a, q).wait_send()

    @pl.loop(0, 3)
    def _(g):
        to_mate(g).wait_send()
        across(g).wait_send()
        to_ymate(g).wait_send()
        for d in range(1, 4):
            scatter(g, d).wait_send()
            spread(g, d).wait_send()


def call_kernel(*args):
    vm = pltpu.VMEM
    dma = pltpu.SemaphoreType.DMA
    whole = pl.BlockSpec(memory_space=pltpu.VMEM)
    return pl.pallas_call(
        kernel,
        name="ocean_block",
        out_shape=(
            jax.ShapeDtypeStruct((32, 16, 256), BF),
            jax.ShapeDtypeStruct((32, 16, 256), BF),
            jax.ShapeDtypeStruct((9, 128, 256), BF),
            jax.ShapeDtypeStruct((9, 256, 128), BF),
        ),
        in_specs=[pl.BlockSpec(memory_space=pl.ANY)] * 4 + [pl.BlockSpec(memory_space=pltpu.SMEM)],
        out_specs=(whole, whole, pl.BlockSpec(memory_space=pl.ANY), pl.BlockSpec(memory_space=pl.ANY)),
        scratch_shapes=[
            vm((256, 16, 256), BF), vm((256, 16, 256), BF), vm((9, 256, 128), BF), vm((9, 128, 256), BF),
            vm((9, 128, 256), BF), vm((9, 256, 128), BF),
            vm((18, 256, 256), BF), vm((18, 256, 256), BF),
            vm((384, 768), BF), vm((384, 768), BF), vm((256, 1152), BF), vm((256, 1152), BF),
            vm((16, 1, 256), F32), vm((4, 512, 128), BF), vm((2, 256, 128), F32), vm((2, 256, 128), BF), vm((2, 2, 256, 128), BF),
            vm((18, 384, 256), BF), vm((18, 384, 256), BF), vm((4, 128, 128), F32), vm((2, 128, 128), F32),
            vm((2, 8, 2, 128, 256), F32),
            vm((2, 8, 2, 128, 256), BF), vm((2, 8, 2, 128, 256), BF),
            vm((2, 8, 2, 64, 256), BF), vm((2, 8, 2, 64, 256), BF),
            vm((2, 8, 2, 32, 256), BF), vm((2, 8, 2, 32, 256), BF),
            vm((2, 16, 32, 256), F32),
            vm((3, 2, 6, 128, 128), F32), vm((3, 6, 128, 128), F32),
            vm((3, 4, 6, 32, 128), F32), vm((3, 4, 6, 32, 128), BF), vm((3, 4, 6, 32, 128), BF),
            vm((3, 6, 32, 128), BF), vm((3, 6, 32, 128), BF),
            vm((3, 4, 6, 32, 128), BF), vm((3, 4, 6, 32, 128), BF),
            dma((2, 4)), dma((2,)), dma((2, 3)), dma((2,)), dma((2,)),
            dma((3, 2, 8)), dma((3, 2, 8)), dma((3,)), dma((3,)), dma((3, 4)), dma((3, 4)), dma((3,)), dma((3,)),
            dma((3, 4)), dma((3, 4)), dma((3,)), dma((3,)),
        ],
        compiler_params=pltpu.CompilerParams(
            collective_id=1, has_side_effects=True, vmem_limit_bytes=60 * 2**20
        ),
        cost_estimate=pl.CostEstimate(flops=14_500_000_000, bytes_accessed=10_000_000, transcendentals=1_000_000),
    )(*args)


def finish_kernel(
    scale, block_in, state_in, gout_in, gin_in, block_out, state_out, gout_out, gin_out, gb, gf, hb, hf, bb, sb, sem,
):
    pieces = [(gout_in, gb, gf, gout_out, n) for n in range(3)] + [(gin_in, hb, hf, gin_out, n) for n in range(3)]
    thirds = [pl.ds(3 * n, 3) for n in range(3)]
    come = [
        pltpu.make_async_copy(src.at[thirds[n]], narrow.at[thirds[n]], sem.at[0, i])
        for i, (src, narrow, _, _, n) in enumerate(pieces)
    ]
    go = [
        pltpu.make_async_copy(wide.at[thirds[n]], dst.at[thirds[n]], sem.at[1, i])
        for i, (_, _, wide, dst, n) in enumerate(pieces)
    ]
    for i, (src, held, dst) in enumerate(((block_in, bb, block_out), (state_in, sb, state_out))):
        come.append(pltpu.make_async_copy(src, held, sem.at[0, 6 + i]))
        go.append(pltpu.make_async_copy(held, dst, sem.at[1, 6 + i]))
    for copy in come:
        copy.start()
    for i, (_, narrow, wide, _, n) in enumerate(pieces):
        come[i].wait()
        wide[thirds[n]] = narrow[thirds[n]].astype(F32) * scale
        go[i].start()
    for i in (6, 7):
        come[i].wait()
        go[i].start()
    for copy in go:
        copy.wait()


def finish(scale, *args):
    anywhere = pl.BlockSpec(memory_space=pl.ANY)
    vm = pltpu.VMEM
    return pl.pallas_call(
        functools.partial(finish_kernel, scale),
        name="widen",
        out_shape=(
            jax.ShapeDtypeStruct((32, 16, 256), BF),
            jax.ShapeDtypeStruct((32, 16, 256), BF),
            jax.ShapeDtypeStruct((9, 128, 256), F32),
            jax.ShapeDtypeStruct((9, 256, 128), F32),
        ),
        in_specs=[anywhere] * 4,
        out_specs=(anywhere,) * 4,
        scratch_shapes=[
            vm((9, 128, 256), BF), vm((9, 128, 256), F32), vm((9, 256, 128), BF), vm((9, 256, 128), F32),
            vm((32, 16, 256), BF), vm((32, 16, 256), BF), pltpu.SemaphoreType.DMA((2, 8)),
        ],
        compiler_params=pltpu.CompilerParams(vmem_limit_bytes=62 * 2**20),
    )(*args)


def shards(ocean_state, cotangent, conv_in, conv_out, tile_mask):
    _, height, breadth = ocean_state.shape
    scale = 1.0 / (height * breadth * lax.axis_size("lon")) ** 0.5
    parts = call_kernel(ocean_state, cotangent, conv_in, conv_out, tile_mask)
    block_out, grad_state, grad_out, grad_in = finish(scale, *parts)
    return (block_out, grad_state, grad_in, grad_out)


def solution(mesh):
    in_specs = (
        P(None, None, "lon"),
        P(None, None, "lon"),
        P(None, None, "filt"),
        P(None, "filt", None),
        P(),
    )
    out_specs = (
        P("filt", None, "lon"),
        P("filt", None, "lon"),
        P(None, None, "filt"),
        P(None, "filt", None),
    )
    return jax.shard_map(shards, mesh=mesh, in_specs=in_specs, out_specs=out_specs, check_vma=False)
```
